32 devices in a mesh: group: 2 (over x), row: 16 (over z, y, core).
Axes of the slice: x: 2, y: 2, z: 4, core: 2. Of those that a mesh axis runs over, the one named last changes fastest.
Arguments:
- specimen: bfloat16 [4, 2, 4096, 2048], P('group', None, 'row'), parts along dimension 0, may hold values from -3 to 3
- probe_field: float32 [4, 256, 256], P('group'), parts along dimension 0, may hold values from -6 to 6
- transfer_phase: float32 [256], replicated, may hold values from -3.140625 to 3.140625
- intensity: bfloat16 [512, 256, 256], P(('group', 'row')), parts along dimension 0, may hold values from 0 to 1
- row_offset: int32 [512], P(('group', 'row')), parts along dimension 0, may hold values from 0 to 255, as said below
- col_offset: int32 [512], P(('group', 'row')), parts along dimension 0, may hold values from 0 to 1792
- counts: int32 [32], P(('group', 'row')), parts along dimension 0, may hold values from 1 to 16, as said below
Outputs:
- specimen_grad: float32 [4, 2, 4096, 2048], P('group', None, 'row'), parts along dimension 0
- probe_grad: float32 [4, 256, 256], P('group'), parts along dimension 0
The draws below stay inside these ranges and needn't reach their ends.
There are 2 independent parts, one for each index of `group`. The reference program is written for one: setup_inputs(seed, part) draws one part's arguments, and reference() takes and returns one part's arrays. A program takes and returns all parts, laid end to end along the dimension named above; an argument that names none is the same for every part. Nothing has to cross between parts.
Inputs may be any that keep to these rules, and one draw needn't show every extreme that they name: `row_offset`: on the last device every row offset is 0; slot 0 of the first device has row offset 256 - 1. The live slots of a device are its first counts entries; some device holds exactly 16.
All inputs are finite; a program needn't handle non-finite values.
Results may differ from the reference program's by a relative error of at most 0.012.
Values may be sent and summed in bfloat16 or wider, within the bound.
No kernel may reach another device: no remote copies, remote signals or barrier semaphores. Data moves between devices by JAX's collectives and lax.ppermute only.
A program may use at most 128 MiB of HBM per device.

```python
import math
import jax
import jax.numpy as jnp
from jax import lax

P_SIZE = 256
S = 2
SR = 256
OC = 2048
CAP = 16
ROWS = 4096
SLOTS = 256
N_ROW = 16


def draw_row_offset(key, part):
    key = jax.random.fold_in(key, 11)
    offsets = jax.random.randint(key, (CAP * N_ROW,), 0, SR)
    device_of = jnp.arange(CAP * N_ROW, dtype=jnp.int32) // CAP
    offsets = jnp.where(device_of == N_ROW - 1, offsets % (SR - P_SIZE + 1), offsets)
    offsets = offsets.at[0].set(SR - 1)
    return offsets.astype(jnp.int32)


def draw_counts(key, part):
    key = jax.random.fold_in(key, 12)
    first_key, second_key = jax.random.split(key)
    loads = 1 + jax.random.randint(first_key, (N_ROW,), 0, CAP)
    heaviest = jax.random.randint(second_key, (), 0, N_ROW)
    loads = jnp.where(jnp.arange(N_ROW, dtype=jnp.int32) == heaviest, CAP, loads)
    return loads.astype(jnp.int32)


def with_ends(values, rng, least, top_value):
    shape = values.shape
    place = [jax.random.randint(jax.random.fold_in(rng, axis), (), 0, shape[axis]) for axis in range(len(shape))]
    values = values.at[tuple(place)].set(least)
    longest = shape.index(max(shape))
    place[longest] = (place[longest] + 1) % shape[longest]
    return values.at[tuple(place)].set(top_value)


def level_of(stream_key, shape, shards, smallest, top_value):
    loudness, own = 1.0, jax.random.fold_in(stream_key, 6)
    for dim, shards_of in shards:
        heights = jnp.exp(jax.random.uniform(jax.random.fold_in(own, dim), (shards_of,), jnp.float32, smallest / len(shards), top_value / len(shards)))
        loudness = loudness * jnp.repeat(heights, shape[dim] // shards_of).reshape([-1 if axis == dim else 1 for axis in range(len(shape))])
    return loudness


def gaussian(key, shape, deviation, reach, cuts=(), kind=jnp.bfloat16):
    values = deviation * jax.random.normal(key, shape, jnp.float32)
    if cuts:
        values = values * level_of(key, shape, cuts, -0.22, 0.18)
    return jnp.clip(values, -reach, reach).astype(kind)


def setup_inputs(seed: int = 0, part: int = 0) -> dict:
    streams_of = jax.random.split(jax.random.key(seed), 8)
    part_keys = jax.random.split(jax.random.fold_in(streams_of[7], part), 8)
    specimen = gaussian(part_keys[0], (2, S, ROWS, OC), 0.5, 3.0, ((2, 16),))
    probe_field = gaussian(part_keys[1], (2, P_SIZE, P_SIZE), 1.0, 6.0, (), jnp.float32)
    transfer_phase = jnp.clip(jax.random.uniform(streams_of[2], (P_SIZE,), jnp.float32, -3.140625, 3.140625), -3.140625, 3.140625)
    intensity = jnp.clip(1.0 * jax.random.uniform(part_keys[3], (SLOTS, P_SIZE, P_SIZE), jnp.float32) ** level_of(part_keys[3], (SLOTS, P_SIZE, P_SIZE), ((0, 16),), -0.2, 0.2), 0.0, 1.0).astype(jnp.bfloat16)
    row_offset = draw_row_offset(jax.random.fold_in(jax.random.fold_in(streams_of[7], part), 71), part)
    col_offset = with_ends(jax.random.randint(part_keys[5], (SLOTS,), 0, OC - P_SIZE + 1), jax.random.fold_in(part_keys[5], 1), 0, OC - P_SIZE).astype(jnp.int32)
    counts = draw_counts(jax.random.fold_in(jax.random.fold_in(streams_of[7], part), 71), part)
    return dict(specimen=specimen, probe_field=probe_field, transfer_phase=transfer_phase, intensity=intensity, row_offset=row_offset, col_offset=col_offset, counts=counts)


def make_tables(transfer_phase, extent):
    indices = jnp.arange(extent, dtype=jnp.int32)
    product = indices[:, None] * indices[None, :] % extent
    angles = product.astype(jnp.float32) * (2.0 * math.pi / extent)
    norming = 1.0 / math.sqrt(extent)
    four_re = jnp.cos(angles) * norming
    four_im = -jnp.sin(angles) * norming
    cos_phase = jnp.cos(transfer_phase)[:, None]
    sin_phase = jnp.sin(transfer_phase)[:, None]
    mid_re = cos_phase * four_re - sin_phase * four_im
    mid_im = cos_phase * four_im + sin_phase * four_re
    highest = lax.Precision.HIGHEST
    prop_re = jnp.dot(four_re, mid_re, precision=highest) + jnp.dot(four_im, mid_im, precision=highest)
    prop_im = jnp.dot(four_re, mid_im, precision=highest) - jnp.dot(four_im, mid_re, precision=highest)
    result = (four_re, four_im, prop_re, prop_im, prop_re.T, prop_im.T)
    return tuple((item.astype(jnp.bfloat16) for item in result))

def complex_dot(left_re, left_im, right_re, right_im):
    real_part = jnp.dot(left_re, right_re, preferred_element_type=jnp.float32) - jnp.dot(left_im, right_im, preferred_element_type=jnp.float32)
    imag_part = jnp.dot(left_re, right_im, preferred_element_type=jnp.float32) + jnp.dot(left_im, right_re, preferred_element_type=jnp.float32)
    return (real_part, imag_part)

def to_bf(value):
    return value.astype(jnp.bfloat16)

def position_terms(window, measured, probe_field, tables):
    four_re, four_im, prop_re, prop_im, tran_re, tran_im = tables
    slices = window.shape[1]
    spec_re = window[0].astype(jnp.float32)
    spec_im = window[1].astype(jnp.float32)
    wave_re = probe_field[0]
    wave_im = probe_field[1]
    waves = []
    exit_re = wave_re
    exit_im = wave_im
    for s in range(slices):
        waves.append((wave_re, wave_im))
        exit_re = wave_re * spec_re[s] - wave_im * spec_im[s]
        exit_im = wave_re * spec_im[s] + wave_im * spec_re[s]
        if s < slices - 1:
            half_re, half_im = complex_dot(prop_re, prop_im, to_bf(exit_re), to_bf(exit_im))
            wave_re, wave_im = complex_dot(to_bf(half_re), to_bf(half_im), tran_re, tran_im)
    half_re, half_im = complex_dot(four_re, four_im, to_bf(exit_re), to_bf(exit_im))
    far_re, far_im = complex_dot(to_bf(half_re), to_bf(half_im), four_re, four_im)
    residual = far_re * far_re + far_im * far_im - measured.astype(jnp.float32)
    chi_re = to_bf(residual * far_re)
    chi_im = to_bf(residual * far_im)
    half_re, half_im = complex_dot(four_re, -four_im, chi_re, chi_im)
    grad_re, grad_im = complex_dot(to_bf(half_re), to_bf(half_im), four_re, -four_im)
    slice_re = [None] * slices
    slice_im = [None] * slices
    back_re = grad_re
    back_im = grad_im
    for s in range(slices - 1, -1, -1):
        wave_re, wave_im = waves[s]
        slice_re[s] = wave_re * grad_re + wave_im * grad_im
        slice_im[s] = wave_re * grad_im - wave_im * grad_re
        back_re = spec_re[s] * grad_re + spec_im[s] * grad_im
        back_im = spec_re[s] * grad_im - spec_im[s] * grad_re
        if s > 0:
            half_re, half_im = complex_dot(tran_re, -tran_im, to_bf(back_re), to_bf(back_im))
            grad_re, grad_im = complex_dot(to_bf(half_re), to_bf(half_im), prop_re, -prop_im)
    tile_grad = jnp.stack([jnp.stack(slice_re), jnp.stack(slice_im)]).astype(jnp.bfloat16)
    return (tile_grad, jnp.stack([back_re, back_im]))

def reference(specimen, probe_field, transfer_phase, intensity, row_offset, col_offset, counts):
    slices = specimen.shape[1]
    extent = probe_field.shape[1]
    tables = make_tables(transfer_phase, extent)
    extended = jnp.concatenate([specimen, jnp.zeros((2, slices, extent, OC), specimen.dtype)], axis=2)
    slot_ids = jnp.arange(SLOTS, dtype=jnp.int32)
    device_of = slot_ids // CAP
    usable = (slot_ids % CAP < counts[device_of]).astype(jnp.float32)
    row_starts = (device_of * SR + row_offset).astype(jnp.int32)
    gradient = jnp.zeros((2, slices, ROWS + extent, OC), jnp.float32)
    probe_sum = jnp.zeros((2, extent, extent), jnp.float32)

    def advance(running, record):
        gradient, probe_sum = running
        row_at, col_at, weight, measured = record
        zero = jnp.int32(0)
        start = (zero, zero, row_at.astype(jnp.int32), col_at.astype(jnp.int32))
        window = lax.dynamic_slice(extended, start, (2, slices, extent, extent))
        tile_grad, probe_term = position_terms(window, measured, probe_field, tables)
        current = lax.dynamic_slice(gradient, start, (2, slices, extent, extent))
        gradient = lax.dynamic_update_slice(gradient, current + weight * tile_grad.astype(jnp.float32), start)
        probe_sum = probe_sum + weight * probe_term
        return ((gradient, probe_sum), None)
    (gradient, probe_sum), unused = lax.scan(advance, (gradient, probe_sum), (row_starts, col_offset, usable, intensity))
    return (gradient[:, :, :ROWS, :], probe_sum)
```

```python
import functools
import math

import jax
import jax.numpy as jnp
import numpy as np
from jax import lax
from jax.experimental import pallas as pl
from jax.experimental.pallas import tpu as pltpu
from jax.sharding import PartitionSpec as P

LANES = 128
BF = jnp.bfloat16
F32 = jnp.float32


def passed_along(value, axis, steps):
    count = lax.axis_size(axis)
    first, last = (max(0, -steps), min(count, count - steps))
    return lax.ppermute(value, axis, [(source, source + steps) for source in range(first, last)])


def fourier(extent):
    indices = np.arange(extent, dtype=np.int64)
    angles = (indices[:, None] * indices[None, :] % extent) * (2.0 * math.pi / extent)
    norming = 1.0 / math.sqrt(extent)
    return (np.cos(angles) * norming).astype(np.float32), (-np.sin(angles) * norming).astype(np.float32)


def block_table(re, im):
    return jnp.concatenate(
        [jnp.concatenate([re, -im], axis=1), jnp.concatenate([im, re], axis=1)], axis=0
    ).astype(BF)


def make_tables(transfer_phase, extent):
    four_re, four_im = (jnp.asarray(item) for item in fourier(extent))
    cos_phase = jnp.cos(transfer_phase)[:, None]
    sin_phase = jnp.sin(transfer_phase)[:, None]
    mid_re = cos_phase * four_re - sin_phase * four_im
    mid_im = cos_phase * four_im + sin_phase * four_re
    highest = lax.Precision.HIGHEST
    prop_re = jnp.dot(four_re, mid_re, precision=highest) + jnp.dot(four_im, mid_im, precision=highest)
    prop_im = jnp.dot(four_re, mid_im, precision=highest) - jnp.dot(four_im, mid_re, precision=highest)
    return (
        block_table(four_re, four_im),
        block_table(four_re, -four_im),
        block_table(prop_re, prop_im),
        block_table(prop_re.T, -prop_im.T),
    )


def product(left, right):
    return jnp.dot(left, right, preferred_element_type=F32)


def beside(stacked):
    half = stacked.shape[0] // 2
    return jnp.concatenate([stacked[:half], stacked[half:]], axis=1).astype(BF)


def stage_kernel(
    plan, stage, *refs
):
    (first_tile, end_tile, final_tile, halo_start, has_past, is_last) = plan
    refs = list(refs)
    row_ref, col_ref, count_ref = refs[:3]
    del refs[:3]
    four_ref, conj_ref, prop_ref, back_ref = refs[:4]
    del refs[:4]
    probe_ref, intensity_ref, specimen_ref = refs[:3]
    del refs[:3]
    halo_now = refs.pop(0)
    if has_past:
        halo_past, carry_in, probe_in, interior_in = refs[:4]
        del refs[:4]
        del interior_in
    interior_ref = refs.pop(0)
    overflow_ref = refs.pop(0) if final_tile > first_tile else None
    carry_out = None if is_last else refs.pop(0)
    probe_out = refs.pop(0)
    (slots_ref, ext_ref, acc_ref, measured_ref, round_ref, twice_ref, sum_ref, win_ref, wave0_ref, wave1_ref,
     stack_ref, tile_ref, load_sem, slot_sem, store_sem) = refs
    extent = probe_ref.shape[1]
    tiles = end_tile - first_tile
    past_tiles = halo_start - first_tile
    own_count = count_ref[0]
    slot_total = row_ref.shape[0]

    copies = []
    for j in range(tiles):
        lanes = pl.ds((first_tile + j) * LANES, LANES)
        copies.append(pltpu.make_async_copy(
            specimen_ref.at[:, :, :, lanes], ext_ref.at[:, :, j, pl.ds(0, extent), :], load_sem.at[2 * j]))
        if j < past_tiles:
            at = halo_past.shape[3] - (past_tiles - j) * LANES
            source = halo_past.at[:, :, :, pl.ds(at, LANES)]
        else:
            source = halo_now.at[:, :, :, pl.ds((j - past_tiles) * LANES, LANES)]
        copies.append(pltpu.make_async_copy(
            source, ext_ref.at[:, :, j, pl.ds(extent, extent), :], load_sem.at[2 * j + 1]))
    for copy in copies:
        copy.start()
    carried = None
    if has_past:
        carried = pltpu.make_async_copy(carry_in, acc_ref.at[:, :, pl.ds(0, past_tiles), :, :], store_sem.at[0])
        carried.start()

    def gather(k, n):
        last = (col_ref[k] + extent - 1) // LANES
        here = (last >= halo_start) & (last < end_tile) & (k < own_count)

        @pl.when(here)
        def _():
            slots_ref[n] = k

        return n + here.astype(jnp.int32)

    n_slots = lax.fori_loop(0, slot_total, gather, jnp.int32(0))

    def fetch(i):
        return pltpu.make_async_copy(
            intensity_ref.at[slots_ref[i]], measured_ref.at[lax.rem(i, 2)], slot_sem.at[lax.rem(i, 2)])

    @pl.when(n_slots > 0)
    def _():
        fetch(0).start()

    for part in range(2):
        for j in range(2):
            block = probe_ref[part, :, j * LANES:(j + 1) * LANES]
            twice_ref[part, j, pl.ds(0, extent), :] = block
            twice_ref[part, j, pl.ds(extent, extent), :] = block
    sum_ref[...] = jnp.zeros_like(sum_ref)
    for j in range(tiles):
        if not (has_past and j < past_tiles):
            acc_ref[:, :, j] = jnp.zeros_like(acc_ref[:, :, j])
    for copy in copies:
        copy.wait()
    if carried is not None:
        carried.wait()

    lane = lax.broadcasted_iota(jnp.int32, (extent, LANES), 1)

    def visit(i, unused):
        slot = slots_ref[i]

        @pl.when(i + 1 < n_slots)
        def _():
            fetch(i + 1).start()

        r = row_ref[slot]
        c = col_ref[slot]
        b = c // LANES
        shift = c - b * LANES
        at0 = b - first_tile
        at1 = at0 + 1
        at2 = jnp.minimum(at0 + 2, tiles - 1)

        def rows_of_window(t, unused):
            own = t * 16
            at = pl.multiple_of(jnp.where(own < r, own + extent, own), 16)
            own = pl.multiple_of(own, 16)
            low = lax.broadcasted_iota(jnp.int32, (16, LANES), 1) < shift
            mixed = (own < r) & (own + 16 > r)
            from_own = lax.broadcasted_iota(jnp.int32, (16, LANES), 0) + own >= r
            for part in range(2):
                for s in range(2):
                    pick = []
                    for j in (at0, at1, at2):
                        far = ext_ref[part, s, j, pl.ds(at, 16), :].astype(F32)
                        near = ext_ref[part, s, j, pl.ds(own, 16), :].astype(F32)
                        pick.append(jnp.where(from_own, near, far))
                    win_ref[part, s, pl.ds(own, 16), 0:LANES] = jnp.where(low, pick[2], pick[0]).astype(BF)
                    win_ref[part, s, pl.ds(own, 16), LANES:2 * LANES] = pick[1].astype(BF)
            return unused

        lax.fori_loop(0, extent // 16, rows_of_window, 0)

        low = lane < shift
        for part in range(2):
            left = pltpu.roll(twice_ref[part, 0, pl.ds(extent - r, extent), :], shift, 1)
            right = pltpu.roll(twice_ref[part, 1, pl.ds(extent - r, extent), :], shift, 1)
            wave0_ref[part, :, 0:LANES] = jnp.where(low, right, left)
            wave0_ref[part, :, LANES:2 * LANES] = jnp.where(low, left, right)

        def leave(wave_ref, s):
            spec_re = win_ref[0, s].astype(F32)
            spec_im = win_ref[1, s].astype(F32)
            wave_re, wave_im = wave_ref[0], wave_ref[1]
            stack_ref[0:extent] = (wave_re * spec_re - wave_im * spec_im).astype(BF)
            stack_ref[extent:2 * extent] = (wave_re * spec_im + wave_im * spec_re).astype(BF)

        def return_through(wave_ref, s, grad):
            grad_re, grad_im = grad[:, :extent], grad[:, extent:]
            wave_re, wave_im = wave_ref[0], wave_ref[1]
            tile_ref[0, s] = (wave_re * grad_re + wave_im * grad_im).astype(BF)
            tile_ref[1, s] = (wave_re * grad_im - wave_im * grad_re).astype(BF)
            spec_re = win_ref[0, s].astype(F32)
            spec_im = win_ref[1, s].astype(F32)
            return spec_re * grad_re + spec_im * grad_im, spec_re * grad_im - spec_im * grad_re

        leave(wave0_ref, 0)
        wave = product(beside(product(prop_ref[...], stack_ref[...])), back_ref[...])
        wave1_ref[0] = wave[:, :extent]
        wave1_ref[1] = wave[:, extent:]
        leave(wave1_ref, 1)
        far = product(beside(product(four_ref[...], stack_ref[...])), conj_ref[...])
        fetch(i).wait()
        far_re, far_im = far[:, :extent], far[:, extent:]
        residual = far_re * far_re + far_im * far_im - measured_ref[lax.rem(i, 2)].astype(F32)
        stack_ref[0:extent] = (residual * far_re).astype(BF)
        stack_ref[extent:2 * extent] = (residual * far_im).astype(BF)
        grad = product(beside(product(conj_ref[...], stack_ref[...])), four_ref[...])
        back_re, back_im = return_through(wave1_ref, 1, grad)
        stack_ref[0:extent] = back_re.astype(BF)
        stack_ref[extent:2 * extent] = back_im.astype(BF)
        grad = product(beside(product(back_ref[...], stack_ref[...])), prop_ref[...])
        back = return_through(wave0_ref, 0, grad)

        unroll = lax.rem(LANES - shift, LANES)
        low = lane < LANES - shift
        for part in range(2):
            left = pltpu.roll(back[part][:, :LANES], unroll, 1)
            right = pltpu.roll(back[part][:, LANES:], unroll, 1)
            rows = pl.ds(extent - r, extent)
            sum_ref[part, 0, rows, :] += jnp.where(low, left, right)
            sum_ref[part, 1, rows, :] += jnp.where(low, right, left)

        def rows_of_tile(t, unused):
            own = pl.multiple_of(t * 16, 16)
            low = lax.broadcasted_iota(jnp.int32, (16, LANES), 1) < shift
            from_own = lax.broadcasted_iota(jnp.int32, (16, LANES), 0) + own >= r

            def add_rows(at, keep):
                for part in range(2):
                    for s in range(2):
                        outer = tile_ref[part, s, pl.ds(own, 16), 0:LANES].astype(F32)
                        inner = tile_ref[part, s, pl.ds(own, 16), LANES:2 * LANES].astype(F32)
                        rows = pl.ds(at, 16)
                        acc_ref[part, s, at0, rows, :] += jnp.where(keep & ~low, outer, 0.0)
                        acc_ref[part, s, at1, rows, :] += jnp.where(keep, inner, 0.0)
                        acc_ref[part, s, at2, rows, :] += jnp.where(keep & low, outer, 0.0)

            @pl.when(own + 16 > r)
            def _():
                add_rows(own, from_own)

            @pl.when(own < r)
            def _():
                add_rows(pl.multiple_of(own + extent, 16), ~from_own)

            return unused

        lax.fori_loop(0, extent // 16, rows_of_tile, 0)
        return unused

    lax.fori_loop(0, n_slots, visit, 0)

    copies = []
    done_tiles = final_tile - first_tile
    for j in range(done_tiles):
        lanes = pl.ds((first_tile + j) * LANES, LANES)
        copies.append(pltpu.make_async_copy(
            acc_ref.at[:, :, j, pl.ds(0, extent), :], interior_ref.at[:, :, :, lanes], load_sem.at[2 * j]))
        copies[-1].start()
        round_ref[:, :, j] = acc_ref[:, :, j, extent:2 * extent, :].astype(BF)
        copies.append(pltpu.make_async_copy(
            round_ref.at[:, :, j], overflow_ref.at[:, :, :, pl.ds(j * LANES, LANES)], load_sem.at[2 * j + 1]))
        copies[-1].start()
    if carry_out is not None:
        copies.append(pltpu.make_async_copy(
            acc_ref.at[:, :, pl.ds(done_tiles, tiles - done_tiles), :, :], carry_out, store_sem.at[0]))
        copies[-1].start()
    for part in range(2):
        for j in range(2):
            term = sum_ref[part, j, 0:extent, :] + sum_ref[part, j, extent:2 * extent, :]
            if has_past:
                term = term + probe_in[part, :, j * LANES:(j + 1) * LANES]
            probe_out[part, :, j * LANES:(j + 1) * LANES] = term
    for copy in copies:
        copy.wait()


def run_stage(stage, ends, meta, tables, probe_field, intensity, specimen, halos, past):
    slices, block_rows, columns = specimen.shape[1:]
    extent = probe_field.shape[1]
    is_last = stage == len(ends) - 1
    has_past = stage > 0
    halo_start = ends[stage - 1] if has_past else 0
    first_tile = max(halo_start - 2, 0) if has_past else 0
    end_tile = ends[stage]
    final_tile = end_tile if is_last else end_tile - 2
    tiles = end_tile - first_tile
    plan = (first_tile, end_tile, final_tile, halo_start, has_past, is_last)
    smem = pl.BlockSpec(memory_space=pltpu.SMEM)
    vmem = pl.BlockSpec(memory_space=pltpu.VMEM)
    hbm = pl.BlockSpec(memory_space=pl.ANY)
    args = [*meta, *tables, probe_field, intensity, specimen, halos[stage]]
    in_specs = [smem] * 3 + [vmem] * 4 + [vmem, hbm, hbm, hbm]
    aliases = {}
    if has_past:
        interior, carry, probe_sum = past
        args += [halos[stage - 1], carry, probe_sum, interior]
        in_specs += [hbm, hbm, vmem, hbm]
        aliases = {len(args) - 1: 0}
    outs = [jax.ShapeDtypeStruct((2, slices, block_rows, columns), F32)]
    out_specs = [hbm]
    if final_tile > first_tile:
        outs.append(jax.ShapeDtypeStruct((2, slices, extent, (final_tile - first_tile) * LANES), BF))
        out_specs.append(hbm)
    if not is_last:
        outs.append(jax.ShapeDtypeStruct((2, slices, end_tile - final_tile, 2 * extent, LANES), F32))
        out_specs.append(hbm)
    outs.append(jax.ShapeDtypeStruct((2, extent, extent), F32))
    out_specs.append(vmem)
    pairs = (2, slices)
    scratch = [
        pltpu.SMEM((meta[0].shape[0],), jnp.int32),
        pltpu.VMEM((*pairs, tiles, 2 * extent, LANES), BF),
        pltpu.VMEM((*pairs, tiles, 2 * extent, LANES), F32),
        pltpu.VMEM((2, extent, extent), BF),
        pltpu.VMEM((*pairs, max(final_tile - first_tile, 1), extent, LANES), BF),
        pltpu.VMEM((2, 2, 2 * extent, LANES), F32),
        pltpu.VMEM((2, 2, 2 * extent, LANES), F32),
        pltpu.VMEM((*pairs, extent, extent), BF),
        pltpu.VMEM((2, extent, extent), F32),
        pltpu.VMEM((2, extent, extent), F32),
        pltpu.VMEM((2 * extent, extent), BF),
        pltpu.VMEM((*pairs, extent, extent), BF),
        pltpu.SemaphoreType.DMA((2 * tiles,)),
        pltpu.SemaphoreType.DMA((2,)),
        pltpu.SemaphoreType.DMA((1,)),
    ]
    results = list(pl.pallas_call(
        functools.partial(stage_kernel, plan, stage),
        out_shape=outs,
        in_specs=in_specs,
        out_specs=out_specs,
        scratch_shapes=scratch,
        input_output_aliases=aliases,
        compiler_params=pltpu.CompilerParams(vmem_limit_bytes=50 * 1024 * 1024),
        cost_estimate=pl.CostEstimate(flops=3 * 10**9, bytes_accessed=8 * 10**6, transcendentals=0),
        name=f"stage{stage}",
    )(*args))
    interior = results.pop(0)
    overflow = results.pop(0) if final_tile > first_tile else None
    carry = None if is_last else results.pop(0)
    return (interior, carry, results.pop(0)), overflow, (first_tile, final_tile)


def add_kernel(held_ref, came_ref, out_ref):
    out_ref[...] = held_ref[...] + came_ref[...].astype(F32)


def add_chunk(interior, came, first_tile):
    _, slices, rows, columns = interior.shape
    tiles = came.shape[3] // LANES
    wide = 2 if tiles % 2 == 0 and first_tile % 2 == 0 else 1
    block = (2, slices, rows, wide * LANES)
    place = pl.BlockSpec(block, lambda j: (0, 0, 0, first_tile // wide + j))
    return pl.pallas_call(
        add_kernel,
        grid=(tiles // wide,),
        out_shape=jax.ShapeDtypeStruct(interior.shape, interior.dtype),
        in_specs=[place, pl.BlockSpec(block, lambda j: (0, 0, 0, j))],
        out_specs=place,
        input_output_aliases={0: 0},
        compiler_params=pltpu.CompilerParams(vmem_limit_bytes=32 * 1024 * 1024),
        name=f"add{first_tile}",
    )(interior, came)


def sum_over(value, axis):
    count = lax.axis_size(axis)
    step = 1
    while step < count:
        mine = value.astype(BF)
        other = lax.ppermute(mine, axis, [(k, k ^ step) for k in range(count)])
        value = mine.astype(F32) + other.astype(F32)
        step *= 2
    return value


def body(ends, specimen, probe_field, transfer_phase, intensity, row_offset, col_offset, counts):
    extent = probe_field.shape[1]
    halos = []
    start = 0
    for end in ends:
        halos.append(passed_along(specimen[:, :, :, start * LANES:end * LANES], "row", -1))
        start = end
    tables = make_tables(transfer_phase, extent)
    meta = (row_offset, col_offset, counts)
    past, came = None, []
    for stage in range(len(ends)):
        past, overflow, span = run_stage(
            stage, ends, meta, tables, probe_field, intensity, specimen, halos, past)
        if overflow is not None:
            came.append((passed_along(overflow, "row", 1), span))
    interior, _, probe_sum = past
    probe_total = sum_over(probe_sum, "row")
    for chunk, span in came:
        interior = add_chunk(interior, chunk, span[0])
    return interior, probe_total


def solution(mesh):
    return jax.shard_map(
        functools.partial(body, (4, 8, 12, 16)),
        mesh=mesh,
        in_specs=(
            P("group", None, "row", None),
            P("group", None, None),
            P(),
            P(("group", "row"), None, None),
            P(("group", "row")),
            P(("group", "row")),
            P(("group", "row")),
        ),
        out_specs=(P("group", None, "row", None), P("group", None, None)),
        check_vma=False,
    )
```

```python
import functools
import math

import jax
import jax.numpy as jnp
import numpy as np
from jax import lax
from jax.experimental import pallas as pl
from jax.experimental.pallas import tpu as pltpu
from jax.sharding import PartitionSpec as P

LANES = 128
BF = jnp.bfloat16
F32 = jnp.float32


def passed_along(value, axis, steps):
    count = lax.axis_size(axis)
    first, last = (max(0, -steps), min(count, count - steps))
    return lax.ppermute(value, axis, [(source, source + steps) for source in range(first, last)])


def fourier(extent):
    indices = np.arange(extent, dtype=np.int64)
    angles = (indices[:, None] * indices[None, :] % extent) * (2.0 * math.pi / extent)
    norming = 1.0 / math.sqrt(extent)
    return (np.cos(angles) * norming).astype(np.float32), (-np.sin(angles) * norming).astype(np.float32)


def block_table(re, im):
    return jnp.concatenate(
        [jnp.concatenate([re, -im], axis=1), jnp.concatenate([im, re], axis=1)], axis=0
    ).astype(BF)


def make_tables(transfer_phase, extent):
    four_re, four_im = (jnp.asarray(item) for item in fourier(extent))
    cos_phase = jnp.cos(transfer_phase)[:, None]
    sin_phase = jnp.sin(transfer_phase)[:, None]
    mid_re = cos_phase * four_re - sin_phase * four_im
    mid_im = cos_phase * four_im + sin_phase * four_re
    highest = lax.Precision.HIGHEST
    prop_re = jnp.dot(four_re, mid_re, precision=highest) + jnp.dot(four_im, mid_im, precision=highest)
    prop_im = jnp.dot(four_re, mid_im, precision=highest) - jnp.dot(four_im, mid_re, precision=highest)
    return (
        block_table(four_re, four_im),
        block_table(four_re, -four_im),
        block_table(prop_re, prop_im),
        block_table(prop_re.T, -prop_im.T),
    )


def product(left, right):
    return jnp.dot(left, right, preferred_element_type=F32)


def beside(stacked):
    half = stacked.shape[0] // 2
    return jnp.concatenate([stacked[:half], stacked[half:]], axis=1).astype(BF)


def stage_kernel(
    plan, stage, *refs
):
    (first_tile, end_tile, final_tile, halo_start, has_past, is_last, group_tile, group_goes_on) = plan
    refs = list(refs)
    row_ref, col_ref, count_ref = refs[:3]
    del refs[:3]
    four_ref, conj_ref, prop_ref, back_ref = refs[:4]
    del refs[:4]
    probe_ref, intensity_ref, specimen_ref = refs[:3]
    del refs[:3]
    halo_now = refs.pop(0)
    if has_past:
        halo_past, carry_in, probe_in = refs[:3]
        del refs[:4]
    if group_goes_on:
        del refs[:1]
    interior_ref = refs.pop(0)
    overflow_ref = refs.pop(0)
    carry_out = None if is_last else refs.pop(0)
    probe_out = refs.pop(0)
    (slots_ref, ext_ref, acc_ref, measured_ref, round_ref, twice_ref, sum_ref, win_ref, wave0_ref, wave1_ref,
     stack_ref, tile_ref, load_sem, slot_sem, store_sem) = refs
    extent = probe_ref.shape[1]
    tiles = end_tile - first_tile
    past_tiles = halo_start - first_tile
    own_count = count_ref[0]
    slot_total = row_ref.shape[0]

    copies = []
    for j in range(tiles):
        lanes = pl.ds((first_tile + j) * LANES, LANES)
        copies.append(pltpu.make_async_copy(
            specimen_ref.at[:, :, :, lanes], ext_ref.at[:, :, j, pl.ds(0, extent), :], load_sem.at[2 * j]))
        if j < past_tiles:
            at = halo_past.shape[3] - (past_tiles - j) * LANES
            source = halo_past.at[:, :, :, pl.ds(at, LANES)]
        else:
            source = halo_now.at[:, :, :, pl.ds((j - past_tiles) * LANES, LANES)]
        copies.append(pltpu.make_async_copy(
            source, ext_ref.at[:, :, j, pl.ds(extent, extent), :], load_sem.at[2 * j + 1]))
    for copy in copies:
        copy.start()
    carried = None
    if has_past:
        carried = pltpu.make_async_copy(carry_in, acc_ref.at[:, :, pl.ds(0, past_tiles), :, :], store_sem.at[0])
        carried.start()

    def gather(k, n):
        last = (col_ref[k] + extent - 1) // LANES
        here = (last >= halo_start) & (last < end_tile) & (k < own_count)

        @pl.when(here)
        def _():
            slots_ref[n] = k

        return n + here.astype(jnp.int32)

    n_slots = lax.fori_loop(0, slot_total, gather, jnp.int32(0))

    def fetch(i):
        return pltpu.make_async_copy(
            intensity_ref.at[slots_ref[i]], measured_ref.at[lax.rem(i, 2)], slot_sem.at[lax.rem(i, 2)])

    @pl.when(n_slots > 0)
    def _():
        fetch(0).start()

    for part in range(2):
        for j in range(2):
            block = probe_ref[part, :, j * LANES:(j + 1) * LANES]
            twice_ref[part, j, pl.ds(0, extent), :] = block
            twice_ref[part, j, pl.ds(extent, extent), :] = block
    sum_ref[...] = jnp.zeros_like(sum_ref)
    for j in range(tiles):
        if not (has_past and j < past_tiles):
            acc_ref[:, :, j] = jnp.zeros_like(acc_ref[:, :, j])
    for copy in copies:
        copy.wait()
    if carried is not None:
        carried.wait()

    lane = lax.broadcasted_iota(jnp.int32, (extent, LANES), 1)

    def visit(i, unused):
        slot = slots_ref[i]

        @pl.when(i + 1 < n_slots)
        def _():
            fetch(i + 1).start()

        r = row_ref[slot]
        c = col_ref[slot]
        b = c // LANES
        shift = c - b * LANES
        at0 = b - first_tile
        at1 = at0 + 1
        at2 = jnp.minimum(at0 + 2, tiles - 1)

        def rows_of_window(t, unused):
            own = t * 16
            at = pl.multiple_of(jnp.where(own < r, own + extent, own), 16)
            own = pl.multiple_of(own, 16)
            low = lax.broadcasted_iota(jnp.int32, (16, LANES), 1) < shift
            mixed = (own < r) & (own + 16 > r)
            from_own = lax.broadcasted_iota(jnp.int32, (16, LANES), 0) + own >= r
            for part in range(2):
                for s in range(2):
                    pick = []
                    for j in (at0, at1, at2):
                        far = ext_ref[part, s, j, pl.ds(at, 16), :].astype(F32)
                        near = ext_ref[part, s, j, pl.ds(own, 16), :].astype(F32)
                        pick.append(jnp.where(from_own, near, far))
                    win_ref[part, s, pl.ds(own, 16), 0:LANES] = jnp.where(low, pick[2], pick[0]).astype(BF)
                    win_ref[part, s, pl.ds(own, 16), LANES:2 * LANES] = pick[1].astype(BF)
            return unused

        lax.fori_loop(0, extent // 16, rows_of_window, 0)

        low = lane < shift
        for part in range(2):
            left = pltpu.roll(twice_ref[part, 0, pl.ds(extent - r, extent), :], shift, 1)
            right = pltpu.roll(twice_ref[part, 1, pl.ds(extent - r, extent), :], shift, 1)
            wave0_ref[part, :, 0:LANES] = jnp.where(low, right, left)
            wave0_ref[part, :, LANES:2 * LANES] = jnp.where(low, left, right)

        def leave(wave_ref, s):
            spec_re = win_ref[0, s].astype(F32)
            spec_im = win_ref[1, s].astype(F32)
            wave_re, wave_im = wave_ref[0], wave_ref[1]
            stack_ref[0:extent] = (wave_re * spec_re - wave_im * spec_im).astype(BF)
            stack_ref[extent:2 * extent] = (wave_re * spec_im + wave_im * spec_re).astype(BF)

        def return_through(wave_ref, s, grad):
            grad_re, grad_im = grad[:, :extent], grad[:, extent:]
            wave_re, wave_im = wave_ref[0], wave_ref[1]
            tile_ref[0, s] = (wave_re * grad_re + wave_im * grad_im).astype(BF)
            tile_ref[1, s] = (wave_re * grad_im - wave_im * grad_re).astype(BF)
            spec_re = win_ref[0, s].astype(F32)
            spec_im = win_ref[1, s].astype(F32)
            return spec_re * grad_re + spec_im * grad_im, spec_re * grad_im - spec_im * grad_re

        leave(wave0_ref, 0)
        wave = product(beside(product(prop_ref[...], stack_ref[...])), back_ref[...])
        wave1_ref[0] = wave[:, :extent]
        wave1_ref[1] = wave[:, extent:]
        leave(wave1_ref, 1)
        far = product(beside(product(four_ref[...], stack_ref[...])), conj_ref[...])
        fetch(i).wait()
        far_re, far_im = far[:, :extent], far[:, extent:]
        residual = far_re * far_re + far_im * far_im - measured_ref[lax.rem(i, 2)].astype(F32)
        stack_ref[0:extent] = (residual * far_re).astype(BF)
        stack_ref[extent:2 * extent] = (residual * far_im).astype(BF)
        grad = product(beside(product(conj_ref[...], stack_ref[...])), four_ref[...])
        back_re, back_im = return_through(wave1_ref, 1, grad)
        stack_ref[0:extent] = back_re.astype(BF)
        stack_ref[extent:2 * extent] = back_im.astype(BF)
        grad = product(beside(product(back_ref[...], stack_ref[...])), prop_ref[...])
        back = return_through(wave0_ref, 0, grad)

        unroll = lax.rem(LANES - shift, LANES)
        low = lane < LANES - shift
        for part in range(2):
            left = pltpu.roll(back[part][:, :LANES], unroll, 1)
            right = pltpu.roll(back[part][:, LANES:], unroll, 1)
            rows = pl.ds(extent - r, extent)
            sum_ref[part, 0, rows, :] += jnp.where(low, left, right)
            sum_ref[part, 1, rows, :] += jnp.where(low, right, left)

        def rows_of_tile(t, unused):
            own = pl.multiple_of(t * 16, 16)
            low = lax.broadcasted_iota(jnp.int32, (16, LANES), 1) < shift
            from_own = lax.broadcasted_iota(jnp.int32, (16, LANES), 0) + own >= r

            def add_rows(at, keep):
                for part in range(2):
                    for s in range(2):
                        outer = tile_ref[part, s, pl.ds(own, 16), 0:LANES].astype(F32)
                        inner = tile_ref[part, s, pl.ds(own, 16), LANES:2 * LANES].astype(F32)
                        rows = pl.ds(at, 16)
                        acc_ref[part, s, at0, rows, :] += jnp.where(keep & ~low, outer, 0.0)
                        acc_ref[part, s, at1, rows, :] += jnp.where(keep, inner, 0.0)
                        acc_ref[part, s, at2, rows, :] += jnp.where(keep & low, outer, 0.0)

            @pl.when(own + 16 > r)
            def _():
                add_rows(own, from_own)

            @pl.when(own < r)
            def _():
                add_rows(pl.multiple_of(own + extent, 16), ~from_own)

            return unused

        lax.fori_loop(0, extent // 16, rows_of_tile, 0)
        return unused

    lax.fori_loop(0, n_slots, visit, 0)

    copies = []
    done_tiles = final_tile - first_tile
    for j in range(done_tiles):
        lanes = pl.ds((first_tile + j) * LANES, LANES)
        copies.append(pltpu.make_async_copy(
            acc_ref.at[:, :, j, pl.ds(0, extent), :], interior_ref.at[:, :, :, lanes], load_sem.at[2 * j]))
        copies[-1].start()
        round_ref[:, :, j] = acc_ref[:, :, j, extent:2 * extent, :].astype(BF)
        copies.append(pltpu.make_async_copy(
            round_ref.at[:, :, j], overflow_ref.at[:, :, :, pl.ds((first_tile - group_tile + j) * LANES, LANES)],
            load_sem.at[2 * j + 1]))
        copies[-1].start()
    if carry_out is not None:
        copies.append(pltpu.make_async_copy(
            acc_ref.at[:, :, pl.ds(done_tiles, tiles - done_tiles), :, :], carry_out, store_sem.at[0]))
        copies[-1].start()
    for part in range(2):
        for j in range(2):
            term = sum_ref[part, j, 0:extent, :] + sum_ref[part, j, extent:2 * extent, :]
            if has_past:
                term = term + probe_in[part, :, j * LANES:(j + 1) * LANES]
            probe_out[part, :, j * LANES:(j + 1) * LANES] = term
    for copy in copies:
        copy.wait()


def run_stage(stage, ends, group, meta, tables, probe_field, intensity, specimen, halos, past):
    slices, block_rows, columns = specimen.shape[1:]
    extent = probe_field.shape[1]
    is_last = stage == len(ends) - 1
    has_past = stage > 0
    halo_start = ends[stage - 1] if has_past else 0
    first_tile = max(halo_start - 2, 0) if has_past else 0
    end_tile = ends[stage]
    final_tile = end_tile if is_last else end_tile - 2
    tiles = end_tile - first_tile
    group_tile, group_end, overflow = group
    group_goes_on = overflow is not None
    plan = (first_tile, end_tile, final_tile, halo_start, has_past, is_last, group_tile, group_goes_on)
    smem = pl.BlockSpec(memory_space=pltpu.SMEM)
    vmem = pl.BlockSpec(memory_space=pltpu.VMEM)
    hbm = pl.BlockSpec(memory_space=pl.ANY)
    args = [*meta, *tables, probe_field, intensity, specimen, halos[stage]]
    in_specs = [smem] * 3 + [vmem] * 4 + [vmem, hbm, hbm, hbm]
    aliases = {}
    if has_past:
        interior, carry, probe_sum = past
        args += [halos[stage - 1], carry, probe_sum, interior]
        in_specs += [hbm, hbm, vmem, hbm]
        aliases = {len(args) - 1: 0}
    if group_goes_on:
        args += [overflow]
        in_specs += [hbm]
        aliases[len(args) - 1] = 1
    outs = [
        jax.ShapeDtypeStruct((2, slices, block_rows, columns), F32),
        jax.ShapeDtypeStruct((2, slices, extent, (group_end - group_tile) * LANES), BF),
    ]
    out_specs = [hbm, hbm]
    if not is_last:
        outs.append(jax.ShapeDtypeStruct((2, slices, end_tile - final_tile, 2 * extent, LANES), F32))
        out_specs.append(hbm)
    outs.append(jax.ShapeDtypeStruct((2, extent, extent), F32))
    out_specs.append(vmem)
    pairs = (2, slices)
    scratch = [
        pltpu.SMEM((meta[0].shape[0],), jnp.int32),
        pltpu.VMEM((*pairs, tiles, 2 * extent, LANES), BF),
        pltpu.VMEM((*pairs, tiles, 2 * extent, LANES), F32),
        pltpu.VMEM((2, extent, extent), BF),
        pltpu.VMEM((*pairs, max(final_tile - first_tile, 1), extent, LANES), BF),
        pltpu.VMEM((2, 2, 2 * extent, LANES), F32),
        pltpu.VMEM((2, 2, 2 * extent, LANES), F32),
        pltpu.VMEM((*pairs, extent, extent), BF),
        pltpu.VMEM((2, extent, extent), F32),
        pltpu.VMEM((2, extent, extent), F32),
        pltpu.VMEM((2 * extent, extent), BF),
        pltpu.VMEM((*pairs, extent, extent), BF),
        pltpu.SemaphoreType.DMA((2 * tiles,)),
        pltpu.SemaphoreType.DMA((2,)),
        pltpu.SemaphoreType.DMA((1,)),
    ]
    results = list(pl.pallas_call(
        functools.partial(stage_kernel, plan, stage),
        out_shape=outs,
        in_specs=in_specs,
        out_specs=out_specs,
        scratch_shapes=scratch,
        input_output_aliases=aliases,
        compiler_params=pltpu.CompilerParams(vmem_limit_bytes=50 * 1024 * 1024),
        cost_estimate=pl.CostEstimate(flops=3 * 10**9, bytes_accessed=8 * 10**6, transcendentals=0),
        name=f"stage{stage}",
    )(*args))
    interior = results.pop(0)
    overflow = results.pop(0)
    carry = None if is_last else results.pop(0)
    return (interior, carry, results.pop(0)), (group_tile, group_end, overflow)


def add_kernel(held_ref, came_ref, out_ref):
    out_ref[...] = held_ref[...] + came_ref[...].astype(F32)


def add_chunk(interior, came, first_tile):
    _, slices, rows, columns = interior.shape
    tiles = came.shape[3] // LANES
    wide = 2 if tiles % 2 == 0 and first_tile % 2 == 0 else 1
    block = (2, slices, rows, wide * LANES)
    place = pl.BlockSpec(block, lambda j: (0, 0, 0, first_tile // wide + j))
    return pl.pallas_call(
        add_kernel,
        grid=(tiles // wide,),
        out_shape=jax.ShapeDtypeStruct(interior.shape, interior.dtype),
        in_specs=[place, pl.BlockSpec(block, lambda j: (0, 0, 0, j))],
        out_specs=place,
        input_output_aliases={0: 0},
        compiler_params=pltpu.CompilerParams(vmem_limit_bytes=32 * 1024 * 1024),
        name=f"add{first_tile}",
    )(interior, came)


def sum_over(value, axis):
    count = lax.axis_size(axis)
    steps = [1 << k for k in range(count.bit_length() - 1)]
    for step in steps[:1] + steps[2:] + steps[1:2]:
        mine = value.astype(BF)
        other = lax.ppermute(mine, axis, [(k, k ^ step) for k in range(count)])
        value = mine.astype(F32) + other.astype(F32)
    return value


def body(ends, sends, specimen, probe_field, transfer_phase, intensity, row_offset, col_offset, counts):
    extent = probe_field.shape[1]
    tables = make_tables(transfer_phase, extent)
    halos, source, start = [], specimen, 0
    for k, end in enumerate(ends):
        piece = source[:, :, :, start * LANES:end * LANES]
        halos.append(passed_along(piece, "row", -1))
        start = end
    meta = (row_offset, col_offset, counts)
    past, came, at = None, [], 0
    for stage in range(len(ends)):
        if stage == 0 or stage - 1 in sends:
            last = min(send for send in sends if send >= stage)
            until = ends[last] if last == len(ends) - 1 else ends[last] - 2
            group = (at, until, None)
        past, group = run_stage(
            stage, ends, group, meta, tables, probe_field, intensity, specimen, halos, past)
        if stage in sends:
            if stage + 1 < len(ends):
                sent, halos[stage + 1] = lax.optimization_barrier((group[2], halos[stage + 1]))
                group = (*group[:2], sent)
            came.append((passed_along(group[2], "row", 1), group[0]))
            at = group[1]
    interior, _, probe_sum = past
    early = came[0][0]
    early, probe_sum = lax.optimization_barrier((early, probe_sum))
    came[0] = (early, came[0][1])
    probe_total = sum_over(probe_sum, "row")
    for chunk, first in came:
        interior = add_chunk(interior, chunk, first)
    return interior, probe_total


def solution(mesh):
    return jax.shard_map(
        functools.partial(body, (5, 10, 16), (1, 2)),
        mesh=mesh,
        in_specs=(
            P("group", None, "row", None),
            P("group", None, None),
            P(),
            P(("group", "row"), None, None),
            P(("group", "row")),
            P(("group", "row")),
            P(("group", "row")),
        ),
        out_specs=(P("group", None, "row", None), P("group", None, None)),
        check_vma=False,
    )
```

```python
import functools
import math

import jax
import jax.numpy as jnp
import numpy as np
from jax import lax
from jax.experimental import pallas as pl
from jax.experimental.pallas import tpu as pltpu
from jax.sharding import PartitionSpec as P

LANES = 128
BF = jnp.bfloat16
F32 = jnp.float32


def passed_along(value, axis, steps):
    count = lax.axis_size(axis)
    first, last = (max(0, -steps), min(count, count - steps))
    return lax.ppermute(value, axis, [(source, source + steps) for source in range(first, last)])


def fourier(extent):
    indices = np.arange(extent, dtype=np.int64)
    angles = (indices[:, None] * indices[None, :] % extent) * (2.0 * math.pi / extent)
    norming = 1.0 / math.sqrt(extent)
    return (np.cos(angles) * norming).astype(np.float32), (-np.sin(angles) * norming).astype(np.float32)


def block_table(re, im):
    return jnp.concatenate(
        [jnp.concatenate([re, -im], axis=1), jnp.concatenate([im, re], axis=1)], axis=0
    ).astype(BF)


def make_tables(transfer_phase, extent):
    four_re, four_im = (jnp.asarray(item) for item in fourier(extent))
    cos_phase = jnp.cos(transfer_phase)[:, None]
    sin_phase = jnp.sin(transfer_phase)[:, None]
    mid_re = cos_phase * four_re - sin_phase * four_im
    mid_im = cos_phase * four_im + sin_phase * four_re
    highest = lax.Precision.HIGHEST
    prop_re = jnp.dot(four_re, mid_re, precision=highest) + jnp.dot(four_im, mid_im, precision=highest)
    prop_im = jnp.dot(four_re, mid_im, precision=highest) - jnp.dot(four_im, mid_re, precision=highest)
    return (
        block_table(four_re, four_im),
        block_table(four_re, -four_im),
        block_table(prop_re, prop_im),
        block_table(prop_re.T, -prop_im.T),
    )


def product(left, right):
    return jnp.dot(left, right, preferred_element_type=F32)


def beside(stacked):
    half = stacked.shape[0] // 2
    return jnp.concatenate([stacked[:half], stacked[half:]], axis=1).astype(BF)


def stage_kernel(
    plan, stage, *refs
):
    (first_tile, end_tile, final_tile, halo_start, has_past, is_last, group_tile, group_goes_on) = plan
    refs = list(refs)
    row_ref, col_ref, count_ref = refs[:3]
    del refs[:3]
    four_ref, conj_ref, prop_ref, back_ref = refs[:4]
    del refs[:4]
    probe_ref, intensity_ref, specimen_ref = refs[:3]
    del refs[:3]
    halo_now = refs.pop(0)
    if has_past:
        halo_past, carry_in, probe_in = refs[:3]
        del refs[:4]
    if group_goes_on:
        del refs[:1]
    interior_ref = refs.pop(0)
    overflow_ref = refs.pop(0)
    carry_out = None if is_last else refs.pop(0)
    probe_out = refs.pop(0)
    (slots_ref, ext_ref, acc_ref, measured_ref, round_ref, twice_ref, sum_ref, win_ref, wave0_ref, wave1_ref,
     stack_ref, half_ref, tile_ref, load_sem, slot_sem, store_sem) = refs
    extent = probe_ref.shape[1]
    tiles = end_tile - first_tile
    past_tiles = halo_start - first_tile
    own_count = count_ref[0]
    slot_total = row_ref.shape[0]

    copies = []
    for j in range(tiles):
        lanes = pl.ds((first_tile + j) * LANES, LANES)
        copies.append(pltpu.make_async_copy(
            specimen_ref.at[:, :, :, lanes], ext_ref.at[:, :, j, pl.ds(0, extent), :], load_sem.at[2 * j]))
        if j < past_tiles:
            at = halo_past.shape[3] - (past_tiles - j) * LANES
            source = halo_past.at[:, :, :, pl.ds(at, LANES)]
        else:
            source = halo_now.at[:, :, :, pl.ds((j - past_tiles) * LANES, LANES)]
        copies.append(pltpu.make_async_copy(
            source, ext_ref.at[:, :, j, pl.ds(extent, extent), :], load_sem.at[2 * j + 1]))
    for copy in copies:
        copy.start()
    carried = None
    if has_past:
        carried = pltpu.make_async_copy(carry_in, acc_ref.at[:, :, pl.ds(0, past_tiles), :, :], store_sem.at[0])
        carried.start()

    def gather(k, n):
        last = (col_ref[k] + extent - 1) // LANES
        here = (last >= halo_start) & (last < end_tile) & (k < own_count)

        @pl.when(here)
        def _():
            slots_ref[n] = k

        return n + here.astype(jnp.int32)

    n_slots = lax.fori_loop(0, slot_total, gather, jnp.int32(0))

    def fetch(i):
        return pltpu.make_async_copy(
            intensity_ref.at[slots_ref[i]], measured_ref.at[lax.rem(i, 4)], slot_sem.at[lax.rem(i, 4)])

    def fetch_pair(i):
        for g in range(2):
            @pl.when(i + g < n_slots)
            def _():
                fetch(i + g).start()

    fetch_pair(0)

    for part in range(2):
        for j in range(2):
            block = probe_ref[part, :, j * LANES:(j + 1) * LANES]
            twice_ref[part, j, pl.ds(0, extent), :] = block
            twice_ref[part, j, pl.ds(extent, extent), :] = block
    sum_ref[...] = jnp.zeros_like(sum_ref)
    for j in range(tiles):
        if not (has_past and j < past_tiles):
            acc_ref[:, :, j] = jnp.zeros_like(acc_ref[:, :, j])
    for copy in copies:
        copy.wait()
    if carried is not None:
        carried.wait()

    lane = lax.broadcasted_iota(jnp.int32, (extent, LANES), 1)

    def visit(i, many):
        places = []
        for g in range(many):
            slot = slots_ref[i + g]
            r = row_ref[slot]
            c = col_ref[slot]
            b = c // LANES
            at0 = b - first_tile
            places.append((r, c - b * LANES, (at0, at0 + 1, jnp.minimum(at0 + 2, tiles - 1))))
        every = range(many)

        def row_starts(r):
            return [pl.multiple_of(jnp.where(t + 16 <= r, t + extent, t), 16) for t in range(0, extent, 16)]

        def masks(r, shift):
            mixed = pl.multiple_of(r // 16 * 16, 16)
            low = lax.broadcasted_iota(jnp.int32, (16, LANES), 1) < shift
            own = lax.broadcasted_iota(jnp.int32, (16, LANES), 0) + mixed >= r
            return mixed, low, own

        def take_window(g):
            r, shift, ats = places[g]
            at0, at1, at2 = ats
            mixed, low, own = masks(r, shift)
            row_at = row_starts(r)
            for part in range(2):
                for s in range(2):
                    for t, at in zip(range(0, extent, 16), row_at):
                        rows = pl.ds(at, 16)
                        win_ref[g, part, s, t:t + 16, 0:LANES] = jnp.where(
                            low, ext_ref[part, s, at2, rows, :], ext_ref[part, s, at0, rows, :])
                        win_ref[g, part, s, t:t + 16, LANES:2 * LANES] = ext_ref[part, s, at1, rows, :]
                    rows, rows_under = pl.ds(mixed, 16), pl.ds(pl.multiple_of(mixed + extent, 16), 16)
                    picked = [jnp.where(own, ext_ref[part, s, at, rows, :], ext_ref[part, s, at, rows_under, :])
                              for at in ats]
                    win_ref[g, part, s, rows, 0:LANES] = jnp.where(low, picked[2], picked[0])
                    win_ref[g, part, s, rows, LANES:2 * LANES] = picked[1]

        def take_probe(g):
            r, shift, _ = places[g]
            low = lane < shift
            for part in range(2):
                left = pltpu.roll(twice_ref[part, 0, pl.ds(extent - r, extent), :], shift, 1)
                right = pltpu.roll(twice_ref[part, 1, pl.ds(extent - r, extent), :], shift, 1)
                wave0_ref[g, part, :, 0:LANES] = jnp.where(low, right, left)
                wave0_ref[g, part, :, LANES:2 * LANES] = jnp.where(low, left, right)

        def put(g, re, im):
            lanes = slice(g * extent, (g + 1) * extent)
            stack_ref[0:extent, lanes] = re.astype(BF)
            stack_ref[extent:2 * extent, lanes] = im.astype(BF)

        def leave(wave_ref, s, g):
            spec_re = win_ref[g, 0, s].astype(F32)
            spec_im = win_ref[g, 1, s].astype(F32)
            wave_re, wave_im = wave_ref[g, 0], wave_ref[g, 1]
            put(g, wave_re * spec_re - wave_im * spec_im, wave_re * spec_im + wave_im * spec_re)

        def return_through(wave_ref, s, g, grad_re, grad_im):
            wave_re, wave_im = wave_ref[g, 0], wave_ref[g, 1]
            tile_ref[g, 0, s] = (wave_re * grad_re + wave_im * grad_im).astype(BF)
            tile_ref[g, 1, s] = (wave_re * grad_im - wave_im * grad_re).astype(BF)
            spec_re = win_ref[g, 0, s].astype(F32)
            spec_im = win_ref[g, 1, s].astype(F32)
            return spec_re * grad_re + spec_im * grad_im, spec_re * grad_im - spec_im * grad_re

        def transform(left_ref, right_ref):
            for g in every:
                half = product(left_ref[...], stack_ref[:, g * extent:(g + 1) * extent])
                half_ref[g * extent:(g + 1) * extent, 0:extent] = half[:extent].astype(BF)
                half_ref[g * extent:(g + 1) * extent, extent:2 * extent] = half[extent:].astype(BF)
            whole = product(half_ref[0:many * extent], right_ref[...])
            return [(whole[g * extent:(g + 1) * extent, :extent], whole[g * extent:(g + 1) * extent, extent:])
                    for g in every]

        def give_probe(g, back):
            r, shift, _ = places[g]
            unroll = lax.rem(LANES - shift, LANES)
            low = lane < LANES - shift
            rows = pl.ds(extent - r, extent)
            for part in range(2):
                left = pltpu.roll(back[part][:, :LANES], unroll, 1)
                right = pltpu.roll(back[part][:, LANES:], unroll, 1)
                sum_ref[part, 0, rows, :] += jnp.where(low, left, right)
                sum_ref[part, 1, rows, :] += jnp.where(low, right, left)

        def give_tile(g, s):
            r, shift, ats = places[g]
            at0, at1, at2 = ats
            mixed, low, own = masks(r, shift)

            def add_rows(part, at, outer, inner):
                rows = pl.ds(at, 16)
                acc_ref[part, s, at0, rows, :] += jnp.where(low, 0.0, outer)
                acc_ref[part, s, at1, rows, :] += inner
                acc_ref[part, s, at2, rows, :] += jnp.where(low, outer, 0.0)

            for part in range(2):
                rows = pl.ds(mixed, 16)
                outer = tile_ref[g, part, s, rows, 0:LANES].astype(F32)
                inner = tile_ref[g, part, s, rows, LANES:2 * LANES].astype(F32)
                add_rows(part, pl.multiple_of(mixed + extent, 16),
                         jnp.where(own, 0.0, outer), jnp.where(own, 0.0, inner))
                tile_ref[g, part, s, rows, 0:LANES] = jnp.where(own, outer, 0.0).astype(BF)
                tile_ref[g, part, s, rows, LANES:2 * LANES] = jnp.where(own, inner, 0.0).astype(BF)
                for t, at in zip(range(0, extent, 16), row_starts(r)):
                    add_rows(part, at, tile_ref[g, part, s, t:t + 16, 0:LANES].astype(F32),
                             tile_ref[g, part, s, t:t + 16, LANES:2 * LANES].astype(F32))

        for g in every:
            take_window(g)
            take_probe(g)
            leave(wave0_ref, 0, g)
        for g, (re, im) in enumerate(transform(prop_ref, back_ref)):
            wave1_ref[g, 0] = re
            wave1_ref[g, 1] = im
            leave(wave1_ref, 1, g)
        far = transform(four_ref, conj_ref)
        for g in every:
            fetch(i + g).wait()
        for g, (re, im) in enumerate(far):
            residual = re * re + im * im - measured_ref[lax.rem(i + g, 4)].astype(F32)
            put(g, residual * re, residual * im)
        for g, (re, im) in enumerate(transform(conj_ref, four_ref)):
            put(g, *return_through(wave1_ref, 1, g, re, im))
        grads = transform(back_ref, prop_ref)
        for g, (re, im) in enumerate(grads):
            give_probe(g, return_through(wave0_ref, 0, g, re, im))
        for g in every:
            for s in range(2):
                give_tile(g, s)

    def visit_pair(p, unused):
        fetch_pair(2 * p + 2)
        visit(2 * p, 2)
        return unused

    lax.fori_loop(0, n_slots // 2, visit_pair, 0)

    @pl.when(lax.rem(n_slots, 2) == 1)
    def _():
        visit(n_slots - 1, 1)

    copies = []
    done_tiles = final_tile - first_tile
    for j in range(done_tiles):
        lanes = pl.ds((first_tile + j) * LANES, LANES)
        copies.append(pltpu.make_async_copy(
            acc_ref.at[:, :, j, pl.ds(0, extent), :], interior_ref.at[:, :, :, lanes], load_sem.at[2 * j]))
        copies[-1].start()
        round_ref[:, :, j] = acc_ref[:, :, j, extent:2 * extent, :].astype(BF)
        copies.append(pltpu.make_async_copy(
            round_ref.at[:, :, j], overflow_ref.at[:, :, :, pl.ds((first_tile - group_tile + j) * LANES, LANES)],
            load_sem.at[2 * j + 1]))
        copies[-1].start()
    if carry_out is not None:
        copies.append(pltpu.make_async_copy(
            acc_ref.at[:, :, pl.ds(done_tiles, tiles - done_tiles), :, :], carry_out, store_sem.at[0]))
        copies[-1].start()
    for part in range(2):
        for j in range(2):
            term = sum_ref[part, j, 0:extent, :] + sum_ref[part, j, extent:2 * extent, :]
            if has_past:
                term = term + probe_in[part, :, j * LANES:(j + 1) * LANES]
            probe_out[part, :, j * LANES:(j + 1) * LANES] = term
    for copy in copies:
        copy.wait()


def run_stage(stage, ends, group, meta, tables, probe_field, intensity, specimen, halos, past):
    slices, block_rows, columns = specimen.shape[1:]
    extent = probe_field.shape[1]
    is_last = stage == len(ends) - 1
    has_past = stage > 0
    halo_start = ends[stage - 1] if has_past else 0
    first_tile = max(halo_start - 2, 0) if has_past else 0
    end_tile = ends[stage]
    final_tile = end_tile if is_last else end_tile - 2
    tiles = end_tile - first_tile
    group_tile, group_end, overflow = group
    group_goes_on = overflow is not None
    plan = (first_tile, end_tile, final_tile, halo_start, has_past, is_last, group_tile, group_goes_on)
    smem = pl.BlockSpec(memory_space=pltpu.SMEM)
    vmem = pl.BlockSpec(memory_space=pltpu.VMEM)
    hbm = pl.BlockSpec(memory_space=pl.ANY)
    args = [*meta, *tables, probe_field, intensity, specimen, halos[stage]]
    in_specs = [smem] * 3 + [vmem] * 4 + [vmem, hbm, hbm, hbm]
    aliases = {}
    if has_past:
        interior, carry, probe_sum = past
        args += [halos[stage - 1], carry, probe_sum, interior]
        in_specs += [hbm, hbm, vmem, hbm]
        aliases = {len(args) - 1: 0}
    if group_goes_on:
        args += [overflow]
        in_specs += [hbm]
        aliases[len(args) - 1] = 1
    outs = [
        jax.ShapeDtypeStruct((2, slices, block_rows, columns), F32),
        jax.ShapeDtypeStruct((2, slices, extent, (group_end - group_tile) * LANES), BF),
    ]
    out_specs = [hbm, hbm]
    if not is_last:
        outs.append(jax.ShapeDtypeStruct((2, slices, end_tile - final_tile, 2 * extent, LANES), F32))
        out_specs.append(hbm)
    outs.append(jax.ShapeDtypeStruct((2, extent, extent), F32))
    out_specs.append(vmem)
    pairs = (2, slices)
    scratch = [
        pltpu.SMEM((meta[0].shape[0],), jnp.int32),
        pltpu.VMEM((*pairs, tiles, 2 * extent, LANES), BF),
        pltpu.VMEM((*pairs, tiles, 2 * extent, LANES), F32),
        pltpu.VMEM((4, extent, extent), BF),
        pltpu.VMEM((*pairs, max(final_tile - first_tile, 1), extent, LANES), BF),
        pltpu.VMEM((2, 2, 2 * extent, LANES), F32),
        pltpu.VMEM((2, 2, 2 * extent, LANES), F32),
        pltpu.VMEM((2, *pairs, extent, extent), BF),
        pltpu.VMEM((2, 2, extent, extent), F32),
        pltpu.VMEM((2, 2, extent, extent), F32),
        pltpu.VMEM((2 * extent, 2 * extent), BF),
        pltpu.VMEM((2 * extent, 2 * extent), BF),
        pltpu.VMEM((2, *pairs, extent, extent), BF),
        pltpu.SemaphoreType.DMA((2 * tiles,)),
        pltpu.SemaphoreType.DMA((4,)),
        pltpu.SemaphoreType.DMA((1,)),
    ]
    results = list(pl.pallas_call(
        functools.partial(stage_kernel, plan, stage),
        out_shape=outs,
        in_specs=in_specs,
        out_specs=out_specs,
        scratch_shapes=scratch,
        input_output_aliases=aliases,
        compiler_params=pltpu.CompilerParams(vmem_limit_bytes=50 * 1024 * 1024),
        cost_estimate=pl.CostEstimate(flops=3 * 10**9, bytes_accessed=8 * 10**6, transcendentals=0),
        name=f"stage{stage}",
    )(*args))
    interior = results.pop(0)
    overflow = results.pop(0)
    carry = None if is_last else results.pop(0)
    return (interior, carry, results.pop(0)), (group_tile, group_end, overflow)


def add_kernel(held_ref, came_ref, out_ref):
    out_ref[...] = held_ref[...] + came_ref[...].astype(F32)


def add_chunk(interior, came, first_tile):
    _, slices, rows, columns = interior.shape
    tiles = came.shape[3] // LANES
    wide = 2 if tiles % 2 == 0 and first_tile % 2 == 0 else 1
    block = (2, slices, rows, wide * LANES)
    place = pl.BlockSpec(block, lambda j: (0, 0, 0, first_tile // wide + j))
    return pl.pallas_call(
        add_kernel,
        grid=(tiles // wide,),
        out_shape=jax.ShapeDtypeStruct(interior.shape, interior.dtype),
        in_specs=[place, pl.BlockSpec(block, lambda j: (0, 0, 0, j))],
        out_specs=place,
        input_output_aliases={0: 0},
        compiler_params=pltpu.CompilerParams(vmem_limit_bytes=32 * 1024 * 1024),
        name=f"add{first_tile}",
    )(interior, came)


def sum_over(value, axis):
    count = lax.axis_size(axis)
    steps = [1 << k for k in range(count.bit_length() - 1)]
    for step in steps[:1] + steps[2:] + steps[1:2]:
        mine = value.astype(BF)
        other = lax.ppermute(mine, axis, [(k, k ^ step) for k in range(count)])
        value = mine.astype(F32) + other.astype(F32)
    return value


def body(ends, sends, specimen, probe_field, transfer_phase, intensity, row_offset, col_offset, counts):
    extent = probe_field.shape[1]
    tables = make_tables(transfer_phase, extent)
    halos, source, start = [], specimen, 0
    for k, end in enumerate(ends):
        piece = source[:, :, :, start * LANES:end * LANES]
        halos.append(passed_along(piece, "row", -1))
        start = end
    meta = (row_offset, col_offset, counts)
    past, came, at = None, [], 0
    for stage in range(len(ends)):
        if stage == 0 or stage - 1 in sends:
            last = min(send for send in sends if send >= stage)
            until = ends[last] if last == len(ends) - 1 else ends[last] - 2
            group = (at, until, None)
        past, group = run_stage(
            stage, ends, group, meta, tables, probe_field, intensity, specimen, halos, past)
        if stage in sends:
            if stage + 1 < len(ends):
                sent, halos[stage + 1] = lax.optimization_barrier((group[2], halos[stage + 1]))
                group = (*group[:2], sent)
            came.append((passed_along(group[2], "row", 1), group[0]))
            at = group[1]
    interior, _, probe_sum = past
    early = came[0][0]
    early, probe_sum = lax.optimization_barrier((early, probe_sum))
    came[0] = (early, came[0][1])
    probe_total = sum_over(probe_sum, "row")
    for chunk, first in came:
        interior = add_chunk(interior, chunk, first)
    return interior, probe_total


def solution(mesh):
    return jax.shard_map(
        functools.partial(body, (5, 10, 16), (1, 2)),
        mesh=mesh,
        in_specs=(
            P("group", None, "row", None),
            P("group", None, None),
            P(),
            P(("group", "row"), None, None),
            P(("group", "row")),
            P(("group", "row")),
            P(("group", "row")),
        ),
        out_specs=(P("group", None, "row", None), P("group", None, None)),
        check_vma=False,
    )
```

```python
import functools
import math

import jax
import jax.numpy as jnp
import numpy as np
from jax import lax
from jax.experimental import pallas as pl
from jax.experimental.pallas import tpu as pltpu
from jax.sharding import PartitionSpec as P

LANES = 128
BF = jnp.bfloat16
F32 = jnp.float32


def passed_along(value, axis, steps):
    count = lax.axis_size(axis)
    first, last = (max(0, -steps), min(count, count - steps))
    return lax.ppermute(value, axis, [(source, source + steps) for source in range(first, last)])


def fourier(extent):
    indices = np.arange(extent, dtype=np.int64)
    angles = (indices[:, None] * indices[None, :] % extent) * (2.0 * math.pi / extent)
    norming = 1.0 / math.sqrt(extent)
    return (np.cos(angles) * norming).astype(np.float32), (-np.sin(angles) * norming).astype(np.float32)


def block_table(re, im):
    return jnp.concatenate(
        [jnp.concatenate([re, -im], axis=1), jnp.concatenate([im, re], axis=1)], axis=0
    ).astype(BF)


def make_tables(transfer_phase, extent):
    four_re, four_im = (jnp.asarray(item) for item in fourier(extent))
    cos_phase = jnp.cos(transfer_phase)[:, None]
    sin_phase = jnp.sin(transfer_phase)[:, None]
    mid_re = cos_phase * four_re - sin_phase * four_im
    mid_im = cos_phase * four_im + sin_phase * four_re
    highest = lax.Precision.HIGHEST
    prop_re = jnp.dot(four_re, mid_re, precision=highest) + jnp.dot(four_im, mid_im, precision=highest)
    prop_im = jnp.dot(four_re, mid_im, precision=highest) - jnp.dot(four_im, mid_re, precision=highest)
    return (
        block_table(four_re, four_im),
        block_table(four_re, -four_im),
        block_table(prop_re, prop_im),
        block_table(prop_re.T, -prop_im.T),
    )


def product(left, right):
    return jnp.dot(left, right, preferred_element_type=F32)


def stage_kernel(
    plan, stage, *refs
):
    (first_tile, end_tile, final_tile, halo_start, has_past, is_last, group_tile, group_goes_on) = plan
    refs = list(refs)
    row_ref, col_ref, count_ref = refs[:3]
    del refs[:3]
    tables_hbm = refs[:4]
    del refs[:4]
    probe_ref, intensity_ref, specimen_ref = refs[:3]
    del refs[:3]
    halo_now = refs.pop(0)
    if has_past:
        halo_past, carry_in, probe_in = refs[:3]
        del refs[:4]
    if group_goes_on:
        del refs[:1]
    interior_ref = refs.pop(0)
    overflow_ref = refs.pop(0)
    carry_out = None if is_last else refs.pop(0)
    probe_out = refs.pop(0)
    (slots_ref, ext_ref, acc_ref, measured_ref, round_ref, twice_ref, sum_ref, win_ref, wave0_ref, wave1_ref,
     stack_ref, half_ref, tile_ref, tables_ref,
     load_sem, slot_sem, store_sem, table_sem) = refs
    four_ref, conj_ref, prop_ref, back_ref = (tables_ref.at[k] for k in range(4))
    extent = probe_ref.shape[1]
    tiles = end_tile - first_tile
    past_tiles = halo_start - first_tile
    own_count = count_ref[0]
    slot_total = row_ref.shape[0]

    copies = []
    for j in range(tiles):
        lanes = pl.ds((first_tile + j) * LANES, LANES)
        copies.append(pltpu.make_async_copy(
            specimen_ref.at[:, :, :, lanes], ext_ref.at[:, :, j, pl.ds(0, extent), :], load_sem.at[2 * j]))
        if j < past_tiles:
            at = halo_past.shape[3] - (past_tiles - j) * LANES
            source = halo_past.at[:, :, :, pl.ds(at, LANES)]
        else:
            source = halo_now.at[:, :, :, pl.ds((j - past_tiles) * LANES, LANES)]
        copies.append(pltpu.make_async_copy(
            source, ext_ref.at[:, :, j, pl.ds(extent, extent), :], load_sem.at[2 * j + 1]))
    for k in range(4):
        copies.append(pltpu.make_async_copy(tables_hbm[k], tables_ref.at[k], table_sem.at[k]))
    for copy in copies:
        copy.start()
    carried = None
    if has_past:
        carried = pltpu.make_async_copy(carry_in, acc_ref.at[:, :, pl.ds(0, past_tiles), :, :], store_sem.at[0])
        carried.start()

    def gather(k, n):
        last = (col_ref[k] + extent - 1) // LANES
        here = (last >= halo_start) & (last < end_tile) & (k < own_count)

        @pl.when(here)
        def _():
            slots_ref[n] = k

        return n + here.astype(jnp.int32)

    n_slots = lax.fori_loop(0, slot_total, gather, jnp.int32(0))

    def fetch(i):
        return pltpu.make_async_copy(
            intensity_ref.at[slots_ref[i]], measured_ref.at[lax.rem(i, 4)], slot_sem.at[lax.rem(i, 4)])

    def fetch_pair(i):
        for g in range(2):
            @pl.when(i + g < n_slots)
            def _():
                fetch(i + g).start()

    fetch_pair(0)

    for part in range(2):
        for j in range(2):
            block = probe_ref[part, :, j * LANES:(j + 1) * LANES]
            twice_ref[part, j, pl.ds(0, extent), :] = block
            twice_ref[part, j, pl.ds(extent, extent), :] = block
    sum_ref[...] = jnp.zeros_like(sum_ref)
    for j in range(tiles):
        if not (has_past and j < past_tiles):
            acc_ref[:, :, j] = jnp.zeros_like(acc_ref[:, :, j])
    for copy in copies:
        copy.wait()
    if carried is not None:
        carried.wait()

    lane = lax.broadcasted_iota(jnp.int32, (extent, LANES), 1)

    def visit(i, many):
        places = []
        for g in range(many):
            slot = slots_ref[i + g]
            r = row_ref[slot]
            c = col_ref[slot]
            b = c // LANES
            at0 = b - first_tile
            places.append((r, c - b * LANES, (at0, at0 + 1, jnp.minimum(at0 + 2, tiles - 1))))
        every = range(many)

        def row_starts(r):
            return [pl.multiple_of(jnp.where(t + 16 <= r, t + extent, t), 16) for t in range(0, extent, 16)]

        def masks(r, shift):
            mixed = pl.multiple_of(r // 16 * 16, 16)
            low = lax.broadcasted_iota(jnp.int32, (16, LANES), 1) < shift
            own = lax.broadcasted_iota(jnp.int32, (16, LANES), 0) + mixed >= r
            return mixed, low, own

        def take_window(g, s):
            r, shift, ats = places[g]
            at0, at1, at2 = ats
            mixed, low, own = masks(r, shift)
            row_at = row_starts(r)
            for part in range(2):
                for t, at in zip(range(0, extent, 16), row_at):
                    rows = pl.ds(at, 16)
                    win_ref[g, part, s, t:t + 16, 0:LANES] = jnp.where(
                        low, ext_ref[part, s, at2, rows, :], ext_ref[part, s, at0, rows, :])
                    win_ref[g, part, s, t:t + 16, LANES:2 * LANES] = ext_ref[part, s, at1, rows, :]
                rows, rows_under = pl.ds(mixed, 16), pl.ds(pl.multiple_of(mixed + extent, 16), 16)
                picked = [jnp.where(own, ext_ref[part, s, at, rows, :], ext_ref[part, s, at, rows_under, :])
                          for at in ats]
                win_ref[g, part, s, rows, 0:LANES] = jnp.where(low, picked[2], picked[0])
                win_ref[g, part, s, rows, LANES:2 * LANES] = picked[1]

        def take_probe(g):
            r, shift, _ = places[g]
            low = lane < shift
            for part in range(2):
                left = pltpu.roll(twice_ref[part, 0, pl.ds(extent - r, extent), :], shift, 1)
                right = pltpu.roll(twice_ref[part, 1, pl.ds(extent - r, extent), :], shift, 1)
                wave0_ref[g, part, :, 0:LANES] = jnp.where(low, right, left)
                wave0_ref[g, part, :, LANES:2 * LANES] = jnp.where(low, left, right)

        def put(g, re, im):
            lanes = slice(g * extent, (g + 1) * extent)
            stack_ref[0:extent, lanes] = re.astype(BF)
            stack_ref[extent:2 * extent, lanes] = im.astype(BF)

        def leave(wave_ref, s, g):
            spec_re = win_ref[g, 0, s].astype(F32)
            spec_im = win_ref[g, 1, s].astype(F32)
            wave_re, wave_im = wave_ref[g, 0], wave_ref[g, 1]
            put(g, wave_re * spec_re - wave_im * spec_im, wave_re * spec_im + wave_im * spec_re)

        def return_through(wave_ref, s, g, grad_re, grad_im):
            wave_re, wave_im = wave_ref[g, 0], wave_ref[g, 1]
            tile_ref[g, 0, s] = (wave_re * grad_re + wave_im * grad_im).astype(BF)
            tile_ref[g, 1, s] = (wave_re * grad_im - wave_im * grad_re).astype(BF)
            spec_re = win_ref[g, 0, s].astype(F32)
            spec_im = win_ref[g, 1, s].astype(F32)
            return spec_re * grad_re + spec_im * grad_im, spec_re * grad_im - spec_im * grad_re

        def transform(left_ref, right_ref, beside=None):
            wide = product(left_ref[...], stack_ref[:, 0:many * extent])
            for g in every:
                half = wide[:, g * extent:(g + 1) * extent]
                half_ref[g * extent:(g + 1) * extent, 0:extent] = half[:extent].astype(BF)
                half_ref[g * extent:(g + 1) * extent, extent:2 * extent] = half[extent:].astype(BF)
                if beside is not None:
                    beside(g)
            whole = product(half_ref[0:many * extent], right_ref[...])
            return [(whole[g * extent:(g + 1) * extent, :extent], whole[g * extent:(g + 1) * extent, extent:])
                    for g in every]

        def give_probe(g, back):
            r, shift, _ = places[g]
            unroll = lax.rem(LANES - shift, LANES)
            low = lane < LANES - shift
            rows = pl.ds(extent - r, extent)
            for part in range(2):
                left = pltpu.roll(back[part][:, :LANES], unroll, 1)
                right = pltpu.roll(back[part][:, LANES:], unroll, 1)
                sum_ref[part, 0, rows, :] += jnp.where(low, left, right)
                sum_ref[part, 1, rows, :] += jnp.where(low, right, left)

        def give_tile(g, s):
            r, shift, ats = places[g]
            at0, at1, at2 = ats
            mixed, low, own = masks(r, shift)

            def add_rows(part, at, outer, inner):
                rows = pl.ds(at, 16)
                acc_ref[part, s, at0, rows, :] += jnp.where(low, 0.0, outer)
                acc_ref[part, s, at1, rows, :] += inner
                acc_ref[part, s, at2, rows, :] += jnp.where(low, outer, 0.0)

            for part in range(2):
                rows = pl.ds(mixed, 16)
                outer = tile_ref[g, part, s, rows, 0:LANES].astype(F32)
                inner = tile_ref[g, part, s, rows, LANES:2 * LANES].astype(F32)
                add_rows(part, pl.multiple_of(mixed + extent, 16),
                         jnp.where(own, 0.0, outer), jnp.where(own, 0.0, inner))
                tile_ref[g, part, s, rows, 0:LANES] = jnp.where(own, outer, 0.0).astype(BF)
                tile_ref[g, part, s, rows, LANES:2 * LANES] = jnp.where(own, inner, 0.0).astype(BF)
                for t, at in zip(range(0, extent, 16), row_starts(r)):
                    add_rows(part, at, tile_ref[g, part, s, t:t + 16, 0:LANES].astype(F32),
                             tile_ref[g, part, s, t:t + 16, LANES:2 * LANES].astype(F32))

        for g in every:
            take_window(g, 0)
            take_probe(g)
            leave(wave0_ref, 0, g)
        for g, (re, im) in enumerate(transform(prop_ref, back_ref, lambda g: take_window(g, 1))):
            wave1_ref[g, 0] = re
            wave1_ref[g, 1] = im
            leave(wave1_ref, 1, g)
        far = transform(four_ref, conj_ref)
        for g in every:
            fetch(i + g).wait()
        for g, (re, im) in enumerate(far):
            residual = re * re + im * im - measured_ref[lax.rem(i + g, 4)].astype(F32)
            put(g, residual * re, residual * im)
        for g, (re, im) in enumerate(transform(conj_ref, four_ref)):
            put(g, *return_through(wave1_ref, 1, g, re, im))
        grads = transform(back_ref, prop_ref, lambda g: give_tile(g, 1))
        for g, (re, im) in enumerate(grads):
            give_probe(g, return_through(wave0_ref, 0, g, re, im))
        for g in every:
            give_tile(g, 0)

    def visit_pair(p, unused):
        fetch_pair(2 * p + 2)
        visit(2 * p, 2)
        return unused

    lax.fori_loop(0, n_slots // 2, visit_pair, 0)

    @pl.when(lax.rem(n_slots, 2) == 1)
    def _():
        visit(n_slots - 1, 1)

    copies = []
    done_tiles = final_tile - first_tile
    for j in range(done_tiles):
        lanes = pl.ds((first_tile + j) * LANES, LANES)
        copies.append(pltpu.make_async_copy(
            acc_ref.at[:, :, j, pl.ds(0, extent), :], interior_ref.at[:, :, :, lanes], load_sem.at[2 * j]))
        copies[-1].start()
        round_ref[:, :, j] = acc_ref[:, :, j, extent:2 * extent, :].astype(BF)
        copies.append(pltpu.make_async_copy(
            round_ref.at[:, :, j], overflow_ref.at[:, :, :, pl.ds((first_tile - group_tile + j) * LANES, LANES)],
            load_sem.at[2 * j + 1]))
        copies[-1].start()
    if carry_out is not None:
        copies.append(pltpu.make_async_copy(
            acc_ref.at[:, :, pl.ds(done_tiles, tiles - done_tiles), :, :], carry_out, store_sem.at[0]))
        copies[-1].start()
    for part in range(2):
        for j in range(2):
            term = sum_ref[part, j, 0:extent, :] + sum_ref[part, j, extent:2 * extent, :]
            if has_past:
                term = term + probe_in[part, :, j * LANES:(j + 1) * LANES]
            probe_out[part, :, j * LANES:(j + 1) * LANES] = term
    for copy in copies:
        copy.wait()


def run_stage(stage, ends, group, meta, tables, probe_field, intensity, specimen, halos, past):
    slices, block_rows, columns = specimen.shape[1:]
    extent = probe_field.shape[1]
    is_last = stage == len(ends) - 1
    has_past = stage > 0
    halo_start = ends[stage - 1] if has_past else 0
    first_tile = max(halo_start - 2, 0) if has_past else 0
    end_tile = ends[stage]
    final_tile = end_tile if is_last else end_tile - 2
    tiles = end_tile - first_tile
    group_tile, group_end, overflow = group
    group_goes_on = overflow is not None
    plan = (first_tile, end_tile, final_tile, halo_start, has_past, is_last, group_tile, group_goes_on)
    smem = pl.BlockSpec(memory_space=pltpu.SMEM)
    vmem = pl.BlockSpec(memory_space=pltpu.VMEM)
    hbm = pl.BlockSpec(memory_space=pl.ANY)
    args = [*meta, *tables, probe_field, intensity, specimen, halos[stage]]
    in_specs = [smem] * 3 + [hbm] * 4 + [vmem, hbm, hbm, hbm]
    aliases = {}
    if has_past:
        interior, carry, probe_sum = past
        args += [halos[stage - 1], carry, probe_sum, interior]
        in_specs += [hbm, hbm, vmem, hbm]
        aliases = {len(args) - 1: 0}
    if group_goes_on:
        args += [overflow]
        in_specs += [hbm]
        aliases[len(args) - 1] = 1
    outs = [
        jax.ShapeDtypeStruct((2, slices, block_rows, columns), F32),
        jax.ShapeDtypeStruct((2, slices, extent, (group_end - group_tile) * LANES), BF),
    ]
    out_specs = [hbm, hbm]
    if not is_last:
        outs.append(jax.ShapeDtypeStruct((2, slices, end_tile - final_tile, 2 * extent, LANES), F32))
        out_specs.append(hbm)
    outs.append(jax.ShapeDtypeStruct((2, extent, extent), F32))
    out_specs.append(vmem)
    pairs = (2, slices)
    scratch = [
        pltpu.SMEM((meta[0].shape[0],), jnp.int32),
        pltpu.VMEM((*pairs, tiles, 2 * extent, LANES), BF),
        pltpu.VMEM((*pairs, tiles, 2 * extent, LANES), F32),
        pltpu.VMEM((4, extent, extent), BF),
        pltpu.VMEM((*pairs, max(final_tile - first_tile, 1), extent, LANES), BF),
        pltpu.VMEM((2, 2, 2 * extent, LANES), F32),
        pltpu.VMEM((2, 2, 2 * extent, LANES), F32),
        pltpu.VMEM((2, *pairs, extent, extent), BF),
        pltpu.VMEM((2, 2, extent, extent), F32),
        pltpu.VMEM((2, 2, extent, extent), F32),
        pltpu.VMEM((2 * extent, 2 * extent), BF),
        pltpu.VMEM((2 * extent, 2 * extent), BF),
        pltpu.VMEM((2, *pairs, extent, extent), BF),
        pltpu.VMEM((4, 2 * extent, 2 * extent), BF),
        pltpu.SemaphoreType.DMA((2 * tiles,)),
        pltpu.SemaphoreType.DMA((4,)),
        pltpu.SemaphoreType.DMA((1,)),
        pltpu.SemaphoreType.DMA((4,)),
    ]
    results = list(pl.pallas_call(
        functools.partial(stage_kernel, plan, stage),
        out_shape=outs,
        in_specs=in_specs,
        out_specs=out_specs,
        scratch_shapes=scratch,
        input_output_aliases=aliases,
        compiler_params=pltpu.CompilerParams(vmem_limit_bytes=56 * 1024 * 1024),
        cost_estimate=pl.CostEstimate(flops=3 * 10**9, bytes_accessed=8 * 10**6, transcendentals=0),
        name=f"stage{stage}",
    )(*args))
    interior = results.pop(0)
    overflow = results.pop(0)
    carry = None if is_last else results.pop(0)
    return (interior, carry, results.pop(0)), (group_tile, group_end, overflow)


def add_kernel(first_tile, tiles, held_ref, came_ref, out_ref, held, came, in_sem, out_sem):
    def copies(j):
        lanes = pl.ds((first_tile + j) * LANES, LANES)
        return (
            pltpu.make_async_copy(held_ref.at[:, :, :, lanes], held.at[j], in_sem.at[2 * j]),
            pltpu.make_async_copy(came_ref.at[:, :, :, pl.ds(j * LANES, LANES)], came.at[j], in_sem.at[2 * j + 1]),
            pltpu.make_async_copy(held.at[j], out_ref.at[:, :, :, lanes], out_sem.at[j]),
        )

    for j in range(tiles):
        for copy in copies(j)[:2]:
            copy.start()
    for j in range(tiles):
        for copy in copies(j)[:2]:
            copy.wait()
        held[j] = held[j] + came[j].astype(F32)
        copies(j)[2].start()
    for j in range(tiles):
        copies(j)[2].wait()


def add_chunk(interior, came, first_tile):
    _, slices, rows, _ = interior.shape
    tiles = came.shape[3] // LANES
    hbm = pl.BlockSpec(memory_space=pl.ANY)
    block = (tiles, 2, slices, rows, LANES)
    return pl.pallas_call(
        functools.partial(add_kernel, first_tile, tiles),
        out_shape=jax.ShapeDtypeStruct(interior.shape, interior.dtype),
        in_specs=[hbm, hbm],
        out_specs=hbm,
        scratch_shapes=[
            pltpu.VMEM(block, F32),
            pltpu.VMEM(block, BF),
            pltpu.SemaphoreType.DMA((2 * tiles,)),
            pltpu.SemaphoreType.DMA((tiles,)),
        ],
        input_output_aliases={0: 0},
        compiler_params=pltpu.CompilerParams(vmem_limit_bytes=56 * 1024 * 1024),
        name=f"add{first_tile}",
    )(interior, came)


def exchanged(value, axis, step):
    return lax.ppermute(value, axis, [(k, k ^ step) for k in range(lax.axis_size(axis))])


def sum_over(value, axis, meanwhile):
    count = lax.axis_size(axis)
    steps = [1 << k for k in range(1, count.bit_length() - 1)]
    odd = lax.rem(lax.axis_index(axis), 2) == 1
    kept, given = jnp.where(odd, value[1], value[0]), jnp.where(odd, value[0], value[1])
    kept = kept.astype(BF).astype(F32) + exchanged(given.astype(BF), axis, 1).astype(F32)
    for n, step in enumerate(steps[1:] + steps[:1]):
        mine = kept.astype(BF)
        kept = mine.astype(F32) + exchanged(mine, axis, step).astype(F32)
        if n == len(steps) - 1:
            kept = meanwhile(kept)
    other = exchanged(kept, axis, 1)
    return jnp.stack([jnp.where(odd, other, kept), jnp.where(odd, kept, other)])


def body(ends, sends, specimen, probe_field, transfer_phase, intensity, row_offset, col_offset, counts):
    extent = probe_field.shape[1]
    tables = make_tables(transfer_phase, extent)
    halos, source, start = [], specimen, 0
    for k, end in enumerate(ends):
        piece = source[:, :, :, start * LANES:end * LANES]
        halos.append(passed_along(piece, "row", -1))
        start = end
    meta = (row_offset, col_offset, counts)
    past, came, at = None, [], 0
    for stage in range(len(ends)):
        if stage == 0 or stage - 1 in sends:
            last = min(send for send in sends if send >= stage)
            until = ends[last] if last == len(ends) - 1 else ends[last] - 2
            group = (at, until, None)
        past, group = run_stage(
            stage, ends, group, meta, tables, probe_field, intensity, specimen, halos, past)
        if stage in sends:
            if stage + 1 < len(ends):
                sent, halos[stage + 1] = lax.optimization_barrier((group[2], halos[stage + 1]))
                group = (*group[:2], sent)
            came.append((passed_along(group[2], "row", 1), group[0]))
            at = group[1]
    interior, _, probe_sum = past
    held = [interior]

    def meanwhile(kept):
        kept, held[0] = lax.optimization_barrier((kept, add_chunk(held[0], *came[0])))
        return kept

    probe_total = sum_over(probe_sum, "row", meanwhile)
    interior = add_chunk(held[0], *came[1])
    return interior, probe_total


def solution(mesh):
    return jax.shard_map(
        functools.partial(body, (5, 10, 13, 16), (2, 3)),
        mesh=mesh,
        in_specs=(
            P("group", None, "row", None),
            P("group", None, None),
            P(),
            P(("group", "row"), None, None),
            P(("group", "row")),
            P(("group", "row")),
            P(("group", "row")),
        ),
        out_specs=(P("group", None, "row", None), P("group", None, None)),
        check_vma=False,
    )
```

```python
import functools
import math

import jax
import jax.numpy as jnp
import numpy as np
from jax import lax
from jax.experimental import pallas as pl
from jax.experimental.pallas import tpu as pltpu
from jax.sharding import PartitionSpec as P

LANES = 128
BF = jnp.bfloat16
F32 = jnp.float32


def passed_along(value, axis, steps):
    count = lax.axis_size(axis)
    first, last = (max(0, -steps), min(count, count - steps))
    return lax.ppermute(value, axis, [(source, source + steps) for source in range(first, last)])


def fourier(extent):
    indices = np.arange(extent, dtype=np.int64)
    angles = (indices[:, None] * indices[None, :] % extent) * (2.0 * math.pi / extent)
    norming = 1.0 / math.sqrt(extent)
    return (np.cos(angles) * norming).astype(np.float32), (-np.sin(angles) * norming).astype(np.float32)


def block_table(re, im):
    return jnp.concatenate(
        [jnp.concatenate([re, -im], axis=1), jnp.concatenate([im, re], axis=1)], axis=0
    ).astype(BF)


def make_tables(transfer_phase, extent):
    four_re, four_im = (jnp.asarray(item) for item in fourier(extent))
    cos_phase = jnp.cos(transfer_phase)[:, None]
    sin_phase = jnp.sin(transfer_phase)[:, None]
    mid_re = cos_phase * four_re - sin_phase * four_im
    mid_im = cos_phase * four_im + sin_phase * four_re
    highest = lax.Precision.HIGHEST
    prop_re = jnp.dot(four_re, mid_re, precision=highest) + jnp.dot(four_im, mid_im, precision=highest)
    prop_im = jnp.dot(four_re, mid_im, precision=highest) - jnp.dot(four_im, mid_re, precision=highest)
    return (
        block_table(four_re, four_im),
        block_table(four_re, -four_im),
        block_table(prop_re, prop_im),
        block_table(prop_re.T, -prop_im.T),
    )


def product(left, right):
    return jnp.dot(left, right, preferred_element_type=F32)


def stage_kernel(
    plan, stage, *refs
):
    (first_tile, end_tile, final_tile, halo_start, has_past, is_last, group_tile, group_goes_on) = plan
    refs = list(refs)
    row_ref, col_ref, count_ref = refs[:3]
    del refs[:3]
    tables_hbm = refs[:4]
    del refs[:4]
    probe_ref, intensity_ref, specimen_ref = refs[:3]
    del refs[:3]
    halo_now = refs.pop(0)
    if has_past:
        halo_past, carry_in, probe_in = refs[:3]
        del refs[:4]
    if group_goes_on:
        del refs[:1]
    interior_ref = refs.pop(0)
    overflow_ref = refs.pop(0)
    carry_out = None if is_last else refs.pop(0)
    probe_out = refs.pop(0)
    (slots_ref, ext_ref, acc_ref, measured_ref, round_ref, twice_ref, sum_ref, win_ref, wave0_ref, wave1_ref,
     stack_ref, half_ref, tile_ref, tables_ref,
     load_sem, slot_sem, store_sem, table_sem) = refs
    four_ref, conj_ref, prop_ref, back_ref = (tables_ref.at[k] for k in range(4))
    extent = probe_ref.shape[1]
    tiles = end_tile - first_tile
    past_tiles = halo_start - first_tile
    own_count = count_ref[0]
    slot_total = row_ref.shape[0]

    copies = []
    for j in range(tiles):
        lanes = pl.ds((first_tile + j) * LANES, LANES)
        copies.append(pltpu.make_async_copy(
            specimen_ref.at[:, :, :, lanes], ext_ref.at[:, :, j, pl.ds(0, extent), :], load_sem.at[2 * j]))
        if j < past_tiles:
            at = halo_past.shape[3] - (past_tiles - j) * LANES
            source = halo_past.at[:, :, :, pl.ds(at, LANES)]
        else:
            source = halo_now.at[:, :, :, pl.ds((j - past_tiles) * LANES, LANES)]
        copies.append(pltpu.make_async_copy(
            source, ext_ref.at[:, :, j, pl.ds(extent, extent), :], load_sem.at[2 * j + 1]))
    for k in range(4):
        copies.append(pltpu.make_async_copy(tables_hbm[k], tables_ref.at[k], table_sem.at[k]))
    for copy in copies:
        copy.start()
    carried = None
    if has_past:
        carried = pltpu.make_async_copy(carry_in, acc_ref.at[:, :, pl.ds(0, past_tiles), :, :], store_sem.at[0])
        carried.start()

    def gather(k, n):
        last = (col_ref[k] + extent - 1) // LANES
        here = (last >= halo_start) & (last < end_tile) & (k < own_count)

        @pl.when(here)
        def _():
            slots_ref[n] = k

        return n + here.astype(jnp.int32)

    n_slots = lax.fori_loop(0, slot_total, gather, jnp.int32(0))

    def fetch(i):
        return pltpu.make_async_copy(
            intensity_ref.at[slots_ref[i]], measured_ref.at[lax.rem(i, 4)], slot_sem.at[lax.rem(i, 4)])

    def fetch_pair(i):
        for g in range(2):
            @pl.when(i + g < n_slots)
            def _():
                fetch(i + g).start()

    fetch_pair(0)

    for part in range(2):
        for j in range(2):
            block = probe_ref[part, :, j * LANES:(j + 1) * LANES]
            twice_ref[part, j, pl.ds(0, extent), :] = block
            twice_ref[part, j, pl.ds(extent, extent), :] = block
    sum_ref[...] = jnp.zeros_like(sum_ref)
    for j in range(tiles):
        if not (has_past and j < past_tiles):
            acc_ref[:, :, j] = jnp.zeros_like(acc_ref[:, :, j])
    for copy in copies:
        copy.wait()
    if carried is not None:
        carried.wait()

    lane = lax.broadcasted_iota(jnp.int32, (extent, LANES), 1)

    def visit(i, many):
        places = []
        for g in range(many):
            slot = slots_ref[i + g]
            r = row_ref[slot]
            c = col_ref[slot]
            b = c // LANES
            at0 = b - first_tile
            places.append((r, c - b * LANES, (at0, at0 + 1, jnp.minimum(at0 + 2, tiles - 1))))
        every = range(many)

        def row_starts(r):
            return [pl.multiple_of(jnp.where(t + 16 <= r, t + extent, t), 16) for t in range(0, extent, 16)]

        def masks(r, shift):
            mixed = pl.multiple_of(r // 16 * 16, 16)
            low = lax.broadcasted_iota(jnp.int32, (16, LANES), 1) < shift
            own = lax.broadcasted_iota(jnp.int32, (16, LANES), 0) + mixed >= r
            return mixed, low, own

        def take_window(g, s):
            r, shift, ats = places[g]
            at0, at1, at2 = ats
            mixed, low, own = masks(r, shift)
            row_at = row_starts(r)
            for part in range(2):
                for t, at in zip(range(0, extent, 16), row_at):
                    rows = pl.ds(at, 16)
                    win_ref[g, part, s, t:t + 16, 0:LANES] = jnp.where(
                        low, ext_ref[part, s, at2, rows, :], ext_ref[part, s, at0, rows, :])
                    win_ref[g, part, s, t:t + 16, LANES:2 * LANES] = ext_ref[part, s, at1, rows, :]
                rows, rows_under = pl.ds(mixed, 16), pl.ds(pl.multiple_of(mixed + extent, 16), 16)
                picked = [jnp.where(own, ext_ref[part, s, at, rows, :], ext_ref[part, s, at, rows_under, :])
                          for at in ats]
                win_ref[g, part, s, rows, 0:LANES] = jnp.where(low, picked[2], picked[0])
                win_ref[g, part, s, rows, LANES:2 * LANES] = picked[1]

        def take_probe(g):
            r, shift, _ = places[g]
            low = lane < shift
            for part in range(2):
                left = pltpu.roll(twice_ref[part, 0, pl.ds(extent - r, extent), :], shift, 1)
                right = pltpu.roll(twice_ref[part, 1, pl.ds(extent - r, extent), :], shift, 1)
                wave0_ref[g, part, :, 0:LANES] = jnp.where(low, right, left)
                wave0_ref[g, part, :, LANES:2 * LANES] = jnp.where(low, left, right)

        def put(g, re, im):
            lanes = slice(g * extent, (g + 1) * extent)
            stack_ref[0:extent, lanes] = re.astype(BF)
            stack_ref[extent:2 * extent, lanes] = im.astype(BF)

        def leave(wave_ref, s, g):
            spec_re = win_ref[g, 0, s].astype(F32)
            spec_im = win_ref[g, 1, s].astype(F32)
            wave_re, wave_im = wave_ref[g, 0], wave_ref[g, 1]
            put(g, wave_re * spec_re - wave_im * spec_im, wave_re * spec_im + wave_im * spec_re)

        def return_through(wave_ref, s, g, grad_re, grad_im):
            wave_re, wave_im = wave_ref[g, 0], wave_ref[g, 1]
            tile_ref[g, 0, s] = (wave_re * grad_re + wave_im * grad_im).astype(BF)
            tile_ref[g, 1, s] = (wave_re * grad_im - wave_im * grad_re).astype(BF)
            spec_re = win_ref[g, 0, s].astype(F32)
            spec_im = win_ref[g, 1, s].astype(F32)
            return spec_re * grad_re + spec_im * grad_im, spec_re * grad_im - spec_im * grad_re

        def transform(left_ref, right_ref, beside=None):
            wide = product(left_ref[...], stack_ref[:, 0:many * extent])
            for g in every:
                half = wide[:, g * extent:(g + 1) * extent]
                half_ref[g * extent:(g + 1) * extent, 0:extent] = half[:extent].astype(BF)
                half_ref[g * extent:(g + 1) * extent, extent:2 * extent] = half[extent:].astype(BF)
                if beside is not None:
                    beside(g)
            whole = product(half_ref[0:many * extent], right_ref[...])
            return [(whole[g * extent:(g + 1) * extent, :extent], whole[g * extent:(g + 1) * extent, extent:])
                    for g in every]

        def give_probe(g, back):
            r, shift, _ = places[g]
            unroll = lax.rem(LANES - shift, LANES)
            low = lane < LANES - shift
            rows = pl.ds(extent - r, extent)
            for part in range(2):
                left = pltpu.roll(back[part][:, :LANES], unroll, 1)
                right = pltpu.roll(back[part][:, LANES:], unroll, 1)
                sum_ref[part, 0, rows, :] += jnp.where(low, left, right)
                sum_ref[part, 1, rows, :] += jnp.where(low, right, left)

        def give_tile(g, s):
            r, shift, ats = places[g]
            at0, at1, at2 = ats
            mixed, low, own = masks(r, shift)

            def add_rows(part, at, outer, inner):
                rows = pl.ds(at, 16)
                acc_ref[part, s, at0, rows, :] += jnp.where(low, 0.0, outer)
                acc_ref[part, s, at1, rows, :] += inner
                acc_ref[part, s, at2, rows, :] += jnp.where(low, outer, 0.0)

            for part in range(2):
                rows = pl.ds(mixed, 16)
                outer = tile_ref[g, part, s, rows, 0:LANES].astype(F32)
                inner = tile_ref[g, part, s, rows, LANES:2 * LANES].astype(F32)
                add_rows(part, pl.multiple_of(mixed + extent, 16),
                         jnp.where(own, 0.0, outer), jnp.where(own, 0.0, inner))
                tile_ref[g, part, s, rows, 0:LANES] = jnp.where(own, outer, 0.0).astype(BF)
                tile_ref[g, part, s, rows, LANES:2 * LANES] = jnp.where(own, inner, 0.0).astype(BF)
                for t, at in zip(range(0, extent, 16), row_starts(r)):
                    add_rows(part, at, tile_ref[g, part, s, t:t + 16, 0:LANES].astype(F32),
                             tile_ref[g, part, s, t:t + 16, LANES:2 * LANES].astype(F32))

        for g in every:
            take_window(g, 0)
            take_probe(g)
            leave(wave0_ref, 0, g)
        for g, (re, im) in enumerate(transform(prop_ref, back_ref, lambda g: take_window(g, 1))):
            wave1_ref[g, 0] = re
            wave1_ref[g, 1] = im
            leave(wave1_ref, 1, g)
        far = transform(four_ref, conj_ref)
        for g in every:
            fetch(i + g).wait()
        for g, (re, im) in enumerate(far):
            residual = re * re + im * im - measured_ref[lax.rem(i + g, 4)].astype(F32)
            put(g, residual * re, residual * im)
        for g, (re, im) in enumerate(transform(conj_ref, four_ref)):
            put(g, *return_through(wave1_ref, 1, g, re, im))
        grads = transform(back_ref, prop_ref, lambda g: give_tile(g, 1))
        for g, (re, im) in enumerate(grads):
            give_probe(g, return_through(wave0_ref, 0, g, re, im))
        for g in every:
            give_tile(g, 0)

    def visit_pair(p, unused):
        fetch_pair(2 * p + 2)
        visit(2 * p, 2)
        return unused

    lax.fori_loop(0, n_slots // 2, visit_pair, 0)

    @pl.when(lax.rem(n_slots, 2) == 1)
    def _():
        visit(n_slots - 1, 1)

    copies = []
    done_tiles = final_tile - first_tile
    for j in range(done_tiles):
        lanes = pl.ds((first_tile + j) * LANES, LANES)
        copies.append(pltpu.make_async_copy(
            acc_ref.at[:, :, j, pl.ds(0, extent), :], interior_ref.at[:, :, :, lanes], load_sem.at[2 * j]))
        copies[-1].start()
        round_ref[:, :, j] = acc_ref[:, :, j, extent:2 * extent, :].astype(BF)
        copies.append(pltpu.make_async_copy(
            round_ref.at[:, :, j], overflow_ref.at[:, :, :, pl.ds((first_tile - group_tile + j) * LANES, LANES)],
            load_sem.at[2 * j + 1]))
        copies[-1].start()
    if carry_out is not None:
        copies.append(pltpu.make_async_copy(
            acc_ref.at[:, :, pl.ds(done_tiles, tiles - done_tiles), :, :], carry_out, store_sem.at[0]))
        copies[-1].start()
    for part in range(2):
        for j in range(2):
            term = sum_ref[part, j, 0:extent, :] + sum_ref[part, j, extent:2 * extent, :]
            if has_past:
                term = term + probe_in[part, :, j * LANES:(j + 1) * LANES]
            probe_out[part, :, j * LANES:(j + 1) * LANES] = term
    for copy in copies:
        copy.wait()


def run_stage(stage, ends, group, meta, tables, probe_field, intensity, specimen, halos, past):
    slices, block_rows, columns = specimen.shape[1:]
    extent = probe_field.shape[1]
    is_last = stage == len(ends) - 1
    has_past = stage > 0
    halo_start = ends[stage - 1] if has_past else 0
    first_tile = max(halo_start - 2, 0) if has_past else 0
    end_tile = ends[stage]
    final_tile = end_tile if is_last else end_tile - 2
    tiles = end_tile - first_tile
    group_tile, group_end, overflow = group
    group_goes_on = overflow is not None
    plan = (first_tile, end_tile, final_tile, halo_start, has_past, is_last, group_tile, group_goes_on)
    smem = pl.BlockSpec(memory_space=pltpu.SMEM)
    vmem = pl.BlockSpec(memory_space=pltpu.VMEM)
    hbm = pl.BlockSpec(memory_space=pltpu.HBM)
    free = pl.BlockSpec(memory_space=pl.ANY)
    args = [*meta, *tables, probe_field, intensity, specimen, halos[stage]]
    in_specs = [smem] * 3 + [hbm] * 4 + [vmem, hbm, hbm, free]
    aliases = {}
    if has_past:
        interior, carry, probe_sum = past
        args += [halos[stage - 1], carry, probe_sum, interior]
        in_specs += [free, hbm, vmem, hbm]
        aliases = {len(args) - 1: 0}
    if group_goes_on:
        args += [overflow]
        in_specs += [hbm]
        aliases[len(args) - 1] = 1
    outs = [
        jax.ShapeDtypeStruct((2, slices, block_rows, columns), F32),
        jax.ShapeDtypeStruct((2, slices, extent, (group_end - group_tile) * LANES), BF),
    ]
    out_specs = [hbm, hbm]
    if not is_last:
        outs.append(jax.ShapeDtypeStruct((2, slices, end_tile - final_tile, 2 * extent, LANES), F32))
        out_specs.append(hbm)
    outs.append(jax.ShapeDtypeStruct((2, extent, extent), F32))
    out_specs.append(vmem)
    pairs = (2, slices)
    scratch = [
        pltpu.SMEM((meta[0].shape[0],), jnp.int32),
        pltpu.VMEM((*pairs, tiles, 2 * extent, LANES), BF),
        pltpu.VMEM((*pairs, tiles, 2 * extent, LANES), F32),
        pltpu.VMEM((4, extent, extent), BF),
        pltpu.VMEM((*pairs, max(final_tile - first_tile, 1), extent, LANES), BF),
        pltpu.VMEM((2, 2, 2 * extent, LANES), F32),
        pltpu.VMEM((2, 2, 2 * extent, LANES), F32),
        pltpu.VMEM((2, *pairs, extent, extent), BF),
        pltpu.VMEM((2, 2, extent, extent), F32),
        pltpu.VMEM((2, 2, extent, extent), F32),
        pltpu.VMEM((2 * extent, 2 * extent), BF),
        pltpu.VMEM((2 * extent, 2 * extent), BF),
        pltpu.VMEM((2, *pairs, extent, extent), BF),
        pltpu.VMEM((4, 2 * extent, 2 * extent), BF),
        pltpu.SemaphoreType.DMA((2 * tiles,)),
        pltpu.SemaphoreType.DMA((4,)),
        pltpu.SemaphoreType.DMA((1,)),
        pltpu.SemaphoreType.DMA((4,)),
    ]
    results = list(pl.pallas_call(
        functools.partial(stage_kernel, plan, stage),
        out_shape=outs,
        in_specs=in_specs,
        out_specs=out_specs,
        scratch_shapes=scratch,
        input_output_aliases=aliases,
        compiler_params=pltpu.CompilerParams(vmem_limit_bytes=56 * 1024 * 1024),
        cost_estimate=pl.CostEstimate(flops=3 * 10**9, bytes_accessed=8 * 10**6, transcendentals=0),
        name=f"stage{stage}",
    )(*args))
    interior = results.pop(0)
    overflow = results.pop(0)
    carry = None if is_last else results.pop(0)
    return (interior, carry, results.pop(0)), (group_tile, group_end, overflow)


def add_kernel(first_tile, tiles, held_ref, came_ref, out_ref, held, came, in_sem, out_sem):
    def copies(j):
        lanes = pl.ds((first_tile + j) * LANES, LANES)
        return (
            pltpu.make_async_copy(held_ref.at[:, :, :, lanes], held.at[j], in_sem.at[2 * j]),
            pltpu.make_async_copy(came_ref.at[:, :, :, pl.ds(j * LANES, LANES)], came.at[j], in_sem.at[2 * j + 1]),
            pltpu.make_async_copy(held.at[j], out_ref.at[:, :, :, lanes], out_sem.at[j]),
        )

    for j in range(tiles):
        for copy in copies(j)[:2]:
            copy.start()
    for j in range(tiles):
        for copy in copies(j)[:2]:
            copy.wait()
        held[j] = held[j] + came[j].astype(F32)
        copies(j)[2].start()
    for j in range(tiles):
        copies(j)[2].wait()


def add_chunk(interior, came, first_tile):
    _, slices, rows, _ = interior.shape
    tiles = came.shape[3] // LANES
    hbm = pl.BlockSpec(memory_space=pltpu.HBM)
    block = (tiles, 2, slices, rows, LANES)
    return pl.pallas_call(
        functools.partial(add_kernel, first_tile, tiles),
        out_shape=jax.ShapeDtypeStruct(interior.shape, interior.dtype),
        in_specs=[hbm, pl.BlockSpec(memory_space=pl.ANY)],
        out_specs=hbm,
        scratch_shapes=[
            pltpu.VMEM(block, F32),
            pltpu.VMEM(block, BF),
            pltpu.SemaphoreType.DMA((2 * tiles,)),
            pltpu.SemaphoreType.DMA((tiles,)),
        ],
        input_output_aliases={0: 0},
        compiler_params=pltpu.CompilerParams(vmem_limit_bytes=56 * 1024 * 1024),
        name=f"add{first_tile}",
    )(interior, came)


def exchanged(value, axis, step):
    return lax.ppermute(value, axis, [(k, k ^ step) for k in range(lax.axis_size(axis))])


def sum_over(value, axis, after_pair, meanwhile):
    count = lax.axis_size(axis)
    steps = [1 << k for k in range(1, count.bit_length() - 1)]
    odd = lax.rem(lax.axis_index(axis), 2) == 1
    kept, given = jnp.where(odd, value[1], value[0]), jnp.where(odd, value[0], value[1])
    kept = kept.astype(BF).astype(F32) + exchanged(given.astype(BF), axis, 1).astype(F32)
    for n, step in enumerate(steps):
        mine = kept.astype(BF)
        if n == 1:
            mine = after_pair(mine)
        kept = mine.astype(F32) + exchanged(mine, axis, step).astype(F32)
        if n == 2:
            kept = meanwhile(kept)
    other = exchanged(kept, axis, 1)
    return jnp.stack([jnp.where(odd, other, kept), jnp.where(odd, kept, other)])


def body(ends, sends, specimen, probe_field, transfer_phase, intensity, row_offset, col_offset, counts):
    extent = probe_field.shape[1]
    tables = make_tables(transfer_phase, extent)
    halos, source, start = [], specimen, 0
    for k, end in enumerate(ends):
        piece = source[:, :, :, start * LANES:end * LANES]
        halos.append(passed_along(piece, "row", -1))
        start = end
    meta = (row_offset, col_offset, counts)
    past, sent, at = None, [], 0
    for stage in range(len(ends)):
        if stage == 0 or stage - 1 in sends:
            last = min(send for send in sends if send >= stage)
            until = ends[last] if last == len(ends) - 1 else ends[last] - 2
            group = (at, until, None)
        past, group = run_stage(
            stage, ends, group, meta, tables, probe_field, intensity, specimen, halos, past)
        if stage in sends:
            if stage + 1 < len(ends):
                ready, halos[stage + 1] = lax.optimization_barrier((group[2], halos[stage + 1]))
                group = (*group[:2], ready)
            sent.append((group[2], group[0]))
            at = group[1]
    interior, _, probe_sum = past
    held = {}

    def after_pair(mine):
        ready, mine = lax.optimization_barrier((sent[1][0], mine))
        held["came"] = passed_along(ready, "row", 1)
        return mine

    def meanwhile(kept):
        first = add_chunk(interior, passed_along(sent[0][0], "row", 1), sent[0][1])
        kept, held["interior"] = lax.optimization_barrier((kept, first))
        return kept

    probe_total = sum_over(probe_sum, "row", after_pair, meanwhile)
    interior = add_chunk(held["interior"], held["came"], sent[1][1])
    return interior, probe_total


def solution(mesh):
    return jax.shard_map(
        functools.partial(body, (6, 12, 16), (1, 2)),
        mesh=mesh,
        in_specs=(
            P("group", None, "row", None),
            P("group", None, None),
            P(),
            P(("group", "row"), None, None),
            P(("group", "row")),
            P(("group", "row")),
            P(("group", "row")),
        ),
        out_specs=(P("group", None, "row", None), P("group", None, None)),
        check_vma=False,
    )
```

```python
import functools
import math

import jax
import jax.numpy as jnp
import numpy as np
from jax import lax
from jax.experimental import pallas as pl
from jax.experimental.pallas import tpu as pltpu
from jax.sharding import PartitionSpec as P

LANES = 128
BF = jnp.bfloat16
F32 = jnp.float32


def passed_along(value, axis, steps):
    count = lax.axis_size(axis)
    first, last = (max(0, -steps), min(count, count - steps))
    return lax.ppermute(value, axis, [(source, source + steps) for source in range(first, last)])


def fourier(extent):
    indices = np.arange(extent, dtype=np.int64)
    angles = (indices[:, None] * indices[None, :] % extent) * (2.0 * math.pi / extent)
    norming = 1.0 / math.sqrt(extent)
    return (np.cos(angles) * norming).astype(np.float32), (-np.sin(angles) * norming).astype(np.float32)


def block_table(re, im):
    return jnp.concatenate(
        [jnp.concatenate([re, -im], axis=1), jnp.concatenate([im, re], axis=1)], axis=0
    ).astype(BF)


def make_tables(transfer_phase, extent):
    four_re, four_im = (jnp.asarray(item) for item in fourier(extent))
    cos_phase = jnp.cos(transfer_phase)[:, None]
    sin_phase = jnp.sin(transfer_phase)[:, None]
    mid_re = cos_phase * four_re - sin_phase * four_im
    mid_im = cos_phase * four_im + sin_phase * four_re
    highest = lax.Precision.HIGHEST
    prop_re = jnp.dot(four_re, mid_re, precision=highest) + jnp.dot(four_im, mid_im, precision=highest)
    prop_im = jnp.dot(four_re, mid_im, precision=highest) - jnp.dot(four_im, mid_re, precision=highest)
    return (
        block_table(four_re, four_im),
        block_table(four_re, -four_im),
        block_table(prop_re, prop_im),
        block_table(prop_re.T, -prop_im.T),
    )


def product(left, right):
    return jnp.dot(left, right, preferred_element_type=F32)


def stage_kernel(
    plan, stage, *refs
):
    (first_tile, end_tile, final_tile, halo_start, has_past, is_last, group_tile, group_goes_on) = plan
    refs = list(refs)
    row_ref, col_ref, count_ref = refs[:3]
    del refs[:3]
    four_ref, conj_ref, prop_ref, back_ref = refs[:4]
    del refs[:4]
    probe_ref, intensity_ref, specimen_ref = refs[:3]
    del refs[:3]
    halo_now = refs.pop(0)
    if has_past:
        halo_past, carry_in, probe_in = refs[:3]
        del refs[:4]
    if group_goes_on:
        del refs[:1]
    interior_ref = refs.pop(0)
    overflow_ref = refs.pop(0)
    carry_out = None if is_last else refs.pop(0)
    probe_out = refs.pop(0)
    (slots_ref, ext_ref, acc_ref, measured_ref, round_ref, twice_ref, sum_ref, win_ref, wave0_ref, wave1_ref,
     stack_ref, half_ref, tile_ref, load_sem, slot_sem, store_sem) = refs
    extent = probe_ref.shape[1]
    tiles = end_tile - first_tile
    past_tiles = halo_start - first_tile
    own_count = count_ref[0]
    slot_total = row_ref.shape[0]

    copies = []
    for j in range(tiles):
        lanes = pl.ds((first_tile + j) * LANES, LANES)
        copies.append(pltpu.make_async_copy(
            specimen_ref.at[:, :, :, lanes], ext_ref.at[:, :, j, pl.ds(0, extent), :], load_sem.at[2 * j]))
        if j < past_tiles:
            at = halo_past.shape[3] - (past_tiles - j) * LANES
            source = halo_past.at[:, :, :, pl.ds(at, LANES)]
        else:
            source = halo_now.at[:, :, :, pl.ds((j - past_tiles) * LANES, LANES)]
        copies.append(pltpu.make_async_copy(
            source, ext_ref.at[:, :, j, pl.ds(extent, extent), :], load_sem.at[2 * j + 1]))
    for copy in copies:
        copy.start()
    carried = None
    if has_past:
        carried = pltpu.make_async_copy(carry_in, acc_ref.at[:, :, pl.ds(0, past_tiles), :, :], store_sem.at[0])
        carried.start()

    def gather(k, n):
        last = (col_ref[k] + extent - 1) // LANES
        here = (last >= halo_start) & (last < end_tile) & (k < own_count)

        @pl.when(here)
        def _():
            slots_ref[n] = k

        return n + here.astype(jnp.int32)

    n_slots = lax.fori_loop(0, slot_total, gather, jnp.int32(0))

    def fetch(i):
        return pltpu.make_async_copy(
            intensity_ref.at[slots_ref[i]], measured_ref.at[lax.rem(i, 4)], slot_sem.at[lax.rem(i, 4)])

    def fetch_pair(i):
        for g in range(2):
            @pl.when(i + g < n_slots)
            def _():
                fetch(i + g).start()

    fetch_pair(0)

    for part in range(2):
        for j in range(2):
            block = probe_ref[part, :, j * LANES:(j + 1) * LANES]
            twice_ref[part, j, pl.ds(0, extent), :] = block
            twice_ref[part, j, pl.ds(extent, extent), :] = block
    sum_ref[...] = jnp.zeros_like(sum_ref)
    for j in range(tiles):
        if not (has_past and j < past_tiles):
            acc_ref[:, :, j] = jnp.zeros_like(acc_ref[:, :, j])
    for copy in copies:
        copy.wait()
    if carried is not None:
        carried.wait()

    lane = lax.broadcasted_iota(jnp.int32, (extent, LANES), 1)

    def visit(i, many):
        places = []
        for g in range(many):
            slot = slots_ref[i + g]
            r = row_ref[slot]
            c = col_ref[slot]
            b = c // LANES
            at0 = b - first_tile
            places.append((r, c - b * LANES, (at0, at0 + 1, jnp.minimum(at0 + 2, tiles - 1))))
        every = range(many)

        def row_starts(r):
            return [pl.multiple_of(jnp.where(t + 16 <= r, t + extent, t), 16) for t in range(0, extent, 16)]

        def masks(r, shift):
            mixed = pl.multiple_of(r // 16 * 16, 16)
            low = lax.broadcasted_iota(jnp.int32, (16, LANES), 1) < shift
            own = lax.broadcasted_iota(jnp.int32, (16, LANES), 0) + mixed >= r
            return mixed, low, own

        def take_window(g, s):
            r, shift, ats = places[g]
            at0, at1, at2 = ats
            mixed, low, own = masks(r, shift)
            row_at = row_starts(r)
            for part in range(2):
                for t, at in zip(range(0, extent, 16), row_at):
                    rows = pl.ds(at, 16)
                    win_ref[g, part, s, t:t + 16, 0:LANES] = jnp.where(
                        low, ext_ref[part, s, at2, rows, :], ext_ref[part, s, at0, rows, :])
                    win_ref[g, part, s, t:t + 16, LANES:2 * LANES] = ext_ref[part, s, at1, rows, :]
                rows, rows_under = pl.ds(mixed, 16), pl.ds(pl.multiple_of(mixed + extent, 16), 16)
                picked = [jnp.where(own, ext_ref[part, s, at, rows, :], ext_ref[part, s, at, rows_under, :])
                          for at in ats]
                win_ref[g, part, s, rows, 0:LANES] = jnp.where(low, picked[2], picked[0])
                win_ref[g, part, s, rows, LANES:2 * LANES] = picked[1]

        def take_probe(g):
            r, shift, _ = places[g]
            low = lane < shift
            for part in range(2):
                left = pltpu.roll(twice_ref[part, 0, pl.ds(extent - r, extent), :], shift, 1)
                right = pltpu.roll(twice_ref[part, 1, pl.ds(extent - r, extent), :], shift, 1)
                wave0_ref[g, part, :, 0:LANES] = jnp.where(low, right, left)
                wave0_ref[g, part, :, LANES:2 * LANES] = jnp.where(low, left, right)

        def put(g, re, im):
            lanes = slice(g * extent, (g + 1) * extent)
            stack_ref[0:extent, lanes] = re.astype(BF)
            stack_ref[extent:2 * extent, lanes] = im.astype(BF)

        def leave(wave_ref, s, g):
            spec_re = win_ref[g, 0, s].astype(F32)
            spec_im = win_ref[g, 1, s].astype(F32)
            wave_re, wave_im = wave_ref[g, 0], wave_ref[g, 1]
            put(g, wave_re * spec_re - wave_im * spec_im, wave_re * spec_im + wave_im * spec_re)

        def return_through(wave_ref, s, g, grad_re, grad_im):
            wave_re, wave_im = wave_ref[g, 0], wave_ref[g, 1]
            tile_ref[g, 0, s] = (wave_re * grad_re + wave_im * grad_im).astype(BF)
            tile_ref[g, 1, s] = (wave_re * grad_im - wave_im * grad_re).astype(BF)
            spec_re = win_ref[g, 0, s].astype(F32)
            spec_im = win_ref[g, 1, s].astype(F32)
            return spec_re * grad_re + spec_im * grad_im, spec_re * grad_im - spec_im * grad_re

        def transform(left_ref, right_ref, beside=None):
            wide = product(left_ref[...], stack_ref[:, 0:many * extent])
            for g in every:
                half = wide[:, g * extent:(g + 1) * extent]
                half_ref[g * extent:(g + 1) * extent, 0:extent] = half[:extent].astype(BF)
                half_ref[g * extent:(g + 1) * extent, extent:2 * extent] = half[extent:].astype(BF)
                if beside is not None:
                    beside(g)
            whole = product(half_ref[0:many * extent], right_ref[...])
            return [(whole[g * extent:(g + 1) * extent, :extent], whole[g * extent:(g + 1) * extent, extent:])
                    for g in every]

        def give_probe(g, back):
            r, shift, _ = places[g]
            unroll = lax.rem(LANES - shift, LANES)
            low = lane < LANES - shift
            rows = pl.ds(extent - r, extent)
            for part in range(2):
                left = pltpu.roll(back[part][:, :LANES], unroll, 1)
                right = pltpu.roll(back[part][:, LANES:], unroll, 1)
                sum_ref[part, 0, rows, :] += jnp.where(low, left, right)
                sum_ref[part, 1, rows, :] += jnp.where(low, right, left)

        def give_tile(g, s):
            r, shift, ats = places[g]
            at0, at1, at2 = ats
            mixed, low, own = masks(r, shift)

            def add_rows(part, at, outer, inner):
                rows = pl.ds(at, 16)
                acc_ref[part, s, at0, rows, :] += jnp.where(low, 0.0, outer)
                acc_ref[part, s, at1, rows, :] += inner
                acc_ref[part, s, at2, rows, :] += jnp.where(low, outer, 0.0)

            for part in range(2):
                rows = pl.ds(mixed, 16)
                outer = tile_ref[g, part, s, rows, 0:LANES].astype(F32)
                inner = tile_ref[g, part, s, rows, LANES:2 * LANES].astype(F32)
                add_rows(part, pl.multiple_of(mixed + extent, 16),
                         jnp.where(own, 0.0, outer), jnp.where(own, 0.0, inner))
                tile_ref[g, part, s, rows, 0:LANES] = jnp.where(own, outer, 0.0).astype(BF)
                tile_ref[g, part, s, rows, LANES:2 * LANES] = jnp.where(own, inner, 0.0).astype(BF)
                for t, at in zip(range(0, extent, 16), row_starts(r)):
                    add_rows(part, at, tile_ref[g, part, s, t:t + 16, 0:LANES].astype(F32),
                             tile_ref[g, part, s, t:t + 16, LANES:2 * LANES].astype(F32))

        for g in every:
            take_window(g, 0)
            take_probe(g)
            leave(wave0_ref, 0, g)
        for g, (re, im) in enumerate(transform(prop_ref, back_ref, lambda g: take_window(g, 1))):
            wave1_ref[g, 0] = re
            wave1_ref[g, 1] = im
            leave(wave1_ref, 1, g)
        far = transform(four_ref, conj_ref)
        for g in every:
            fetch(i + g).wait()
        for g, (re, im) in enumerate(far):
            residual = re * re + im * im - measured_ref[lax.rem(i + g, 4)].astype(F32)
            put(g, residual * re, residual * im)
        for g, (re, im) in enumerate(transform(conj_ref, four_ref)):
            put(g, *return_through(wave1_ref, 1, g, re, im))
        grads = transform(back_ref, prop_ref, lambda g: give_tile(g, 1))
        for g, (re, im) in enumerate(grads):
            give_probe(g, return_through(wave0_ref, 0, g, re, im))
        for g in every:
            give_tile(g, 0)

    def visit_pair(p, unused):
        fetch_pair(2 * p + 2)
        visit(2 * p, 2)
        return unused

    lax.fori_loop(0, n_slots // 2, visit_pair, 0)

    @pl.when(lax.rem(n_slots, 2) == 1)
    def _():
        visit(n_slots - 1, 1)

    copies = []
    done_tiles = final_tile - first_tile
    for j in range(done_tiles):
        lanes = pl.ds((first_tile + j) * LANES, LANES)
        copies.append(pltpu.make_async_copy(
            acc_ref.at[:, :, j, pl.ds(0, extent), :], interior_ref.at[:, :, :, lanes], load_sem.at[2 * j]))
        copies[-1].start()
        round_ref[:, :, j] = acc_ref[:, :, j, extent:2 * extent, :].astype(BF)
        copies.append(pltpu.make_async_copy(
            round_ref.at[:, :, j], overflow_ref.at[:, :, :, pl.ds((first_tile - group_tile + j) * LANES, LANES)],
            load_sem.at[2 * j + 1]))
        copies[-1].start()
    if carry_out is not None:
        copies.append(pltpu.make_async_copy(
            acc_ref.at[:, :, pl.ds(done_tiles, tiles - done_tiles), :, :], carry_out, store_sem.at[0]))
        copies[-1].start()
    for part in range(2):
        for j in range(2):
            term = sum_ref[part, j, 0:extent, :] + sum_ref[part, j, extent:2 * extent, :]
            if has_past:
                term = term + probe_in[part, :, j * LANES:(j + 1) * LANES]
            probe_out[part, :, j * LANES:(j + 1) * LANES] = term
    for copy in copies:
        copy.wait()


def run_stage(stage, ends, group, meta, tables, probe_field, intensity, specimen, halos, past):
    slices, block_rows, columns = specimen.shape[1:]
    extent = probe_field.shape[1]
    is_last = stage == len(ends) - 1
    has_past = stage > 0
    halo_start = ends[stage - 1] if has_past else 0
    first_tile = max(halo_start - 2, 0) if has_past else 0
    end_tile = ends[stage]
    final_tile = end_tile if is_last else end_tile - 2
    tiles = end_tile - first_tile
    group_tile, group_end, overflow = group
    group_goes_on = overflow is not None
    plan = (first_tile, end_tile, final_tile, halo_start, has_past, is_last, group_tile, group_goes_on)
    smem = pl.BlockSpec(memory_space=pltpu.SMEM)
    vmem = pl.BlockSpec(memory_space=pltpu.VMEM)
    hbm = pl.BlockSpec(memory_space=pltpu.HBM)
    free = pl.BlockSpec(memory_space=pl.ANY)
    args = [*meta, *tables, probe_field, intensity, specimen, halos[stage]]
    in_specs = [smem] * 3 + [vmem] * 4 + [vmem, hbm, hbm, free]
    aliases = {}
    if has_past:
        interior, carry, probe_sum = past
        args += [halos[stage - 1], carry, probe_sum, interior]
        in_specs += [free, hbm, vmem, hbm]
        aliases = {len(args) - 1: 0}
    if group_goes_on:
        args += [overflow]
        in_specs += [hbm]
        aliases[len(args) - 1] = 1
    outs = [
        jax.ShapeDtypeStruct((2, slices, block_rows, columns), F32),
        jax.ShapeDtypeStruct((2, slices, extent, (group_end - group_tile) * LANES), BF),
    ]
    out_specs = [hbm, hbm]
    if not is_last:
        outs.append(jax.ShapeDtypeStruct((2, slices, end_tile - final_tile, 2 * extent, LANES), F32))
        out_specs.append(hbm)
    outs.append(jax.ShapeDtypeStruct((2, extent, extent), F32))
    out_specs.append(vmem)
    pairs = (2, slices)
    scratch = [
        pltpu.SMEM((meta[0].shape[0],), jnp.int32),
        pltpu.VMEM((*pairs, tiles, 2 * extent, LANES), BF),
        pltpu.VMEM((*pairs, tiles, 2 * extent, LANES), F32),
        pltpu.VMEM((4, extent, extent), BF),
        pltpu.VMEM((*pairs, max(final_tile - first_tile, 1), extent, LANES), BF),
        pltpu.VMEM((2, 2, 2 * extent, LANES), F32),
        pltpu.VMEM((2, 2, 2 * extent, LANES), F32),
        pltpu.VMEM((2, *pairs, extent, extent), BF),
        pltpu.VMEM((2, 2, extent, extent), F32),
        pltpu.VMEM((2, 2, extent, extent), F32),
        pltpu.VMEM((2 * extent, 2 * extent), BF),
        pltpu.VMEM((2 * extent, 2 * extent), BF),
        pltpu.VMEM((2, *pairs, extent, extent), BF),
        pltpu.SemaphoreType.DMA((2 * tiles,)),
        pltpu.SemaphoreType.DMA((4,)),
        pltpu.SemaphoreType.DMA((1,)),
    ]
    results = list(pl.pallas_call(
        functools.partial(stage_kernel, plan, stage),
        out_shape=outs,
        in_specs=in_specs,
        out_specs=out_specs,
        scratch_shapes=scratch,
        input_output_aliases=aliases,
        compiler_params=pltpu.CompilerParams(vmem_limit_bytes=50 * 1024 * 1024),
        cost_estimate=pl.CostEstimate(flops=3 * 10**9, bytes_accessed=8 * 10**6, transcendentals=0),
        name=f"stage{stage}",
    )(*args))
    interior = results.pop(0)
    overflow = results.pop(0)
    carry = None if is_last else results.pop(0)
    return (interior, carry, results.pop(0)), (group_tile, group_end, overflow)


def add_kernel(first_tile, tiles, held_ref, came_ref, out_ref, held, came, in_sem, out_sem):
    def copies(j):
        lanes = pl.ds((first_tile + j) * LANES, LANES)
        return (
            pltpu.make_async_copy(held_ref.at[:, :, :, lanes], held.at[j], in_sem.at[2 * j]),
            pltpu.make_async_copy(came_ref.at[:, :, :, pl.ds(j * LANES, LANES)], came.at[j], in_sem.at[2 * j + 1]),
            pltpu.make_async_copy(held.at[j], out_ref.at[:, :, :, lanes], out_sem.at[j]),
        )

    for j in range(tiles):
        for copy in copies(j)[:2]:
            copy.start()
    for j in range(tiles):
        for copy in copies(j)[:2]:
            copy.wait()
        held[j] = held[j] + came[j].astype(F32)
        copies(j)[2].start()
    for j in range(tiles):
        copies(j)[2].wait()


def add_chunk(interior, came, first_tile):
    _, slices, rows, _ = interior.shape
    tiles = came.shape[3] // LANES
    hbm = pl.BlockSpec(memory_space=pltpu.HBM)
    block = (tiles, 2, slices, rows, LANES)
    return pl.pallas_call(
        functools.partial(add_kernel, first_tile, tiles),
        out_shape=jax.ShapeDtypeStruct(interior.shape, interior.dtype),
        in_specs=[hbm, pl.BlockSpec(memory_space=pl.ANY)],
        out_specs=hbm,
        scratch_shapes=[
            pltpu.VMEM(block, F32),
            pltpu.VMEM(block, BF),
            pltpu.SemaphoreType.DMA((2 * tiles,)),
            pltpu.SemaphoreType.DMA((tiles,)),
        ],
        input_output_aliases={0: 0},
        compiler_params=pltpu.CompilerParams(vmem_limit_bytes=50 * 1024 * 1024),
        name=f"add{first_tile}",
    )(interior, came)


def exchanged(value, axis, step):
    return lax.ppermute(value, axis, [(k, k ^ step) for k in range(lax.axis_size(axis))])


def sum_over(value, axis):
    count = lax.axis_size(axis)
    steps = [1 << k for k in range(1, count.bit_length() - 1)]
    odd = lax.rem(lax.axis_index(axis), 2) == 1
    kept, given = jnp.where(odd, value[1], value[0]), jnp.where(odd, value[0], value[1])
    kept = kept.astype(BF).astype(F32) + exchanged(given.astype(BF), axis, 1).astype(F32)
    for step in steps[1:] + steps[:1]:
        mine = kept.astype(BF)
        kept = mine.astype(F32) + exchanged(mine, axis, step).astype(F32)
    other = exchanged(kept, axis, 1)
    return jnp.stack([jnp.where(odd, other, kept), jnp.where(odd, kept, other)])


def body(ends, sends, specimen, probe_field, transfer_phase, intensity, row_offset, col_offset, counts):
    extent = probe_field.shape[1]
    tables = make_tables(transfer_phase, extent)
    halos, source, start = [], specimen, 0
    for k, end in enumerate(ends):
        piece = source[:, :, :, start * LANES:end * LANES]
        halos.append(passed_along(piece, "row", -1))
        start = end
    meta = (row_offset, col_offset, counts)
    past, sent, at = None, [], 0
    for stage in range(len(ends)):
        if stage == 0 or stage - 1 in sends:
            last = min(send for send in sends if send >= stage)
            until = ends[last] if last == len(ends) - 1 else ends[last] - 2
            group = (at, until, None)
        past, group = run_stage(
            stage, ends, group, meta, tables, probe_field, intensity, specimen, halos, past)
        if stage in sends:
            if stage + 1 < len(ends):
                ready, halos[stage + 1] = lax.optimization_barrier((group[2], halos[stage + 1]))
                group = (*group[:2], ready)
            sent.append((group[2], group[0]))
            at = group[1]
    interior, _, probe_sum = past
    came = [(passed_along(chunk, "row", 1), first) for chunk, first in sent]
    interior = add_chunk(interior, *came[0])
    interior, probe_sum = lax.optimization_barrier((interior, probe_sum))
    probe_total = sum_over(probe_sum, "row")
    interior = add_chunk(interior, *came[1])
    return interior, probe_total


def solution(mesh):
    return jax.shard_map(
        functools.partial(body, (5, 10, 16), (1, 2)),
        mesh=mesh,
        in_specs=(
            P("group", None, "row", None),
            P("group", None, None),
            P(),
            P(("group", "row"), None, None),
            P(("group", "row")),
            P(("group", "row")),
            P(("group", "row")),
        ),
        out_specs=(P("group", None, "row", None), P("group", None, None)),
        check_vma=False,
    )
```

```python
import functools
import math

import jax
import jax.numpy as jnp
import numpy as np
from jax import lax
from jax.experimental import pallas as pl
from jax.experimental.pallas import tpu as pltpu
from jax.sharding import PartitionSpec as P

LANES = 128
BF = jnp.bfloat16
F32 = jnp.float32


def passed_along(value, axis, steps):
    count = lax.axis_size(axis)
    first, last = (max(0, -steps), min(count, count - steps))
    return lax.ppermute(value, axis, [(source, source + steps) for source in range(first, last)])


def fourier(extent):
    indices = np.arange(extent, dtype=np.int64)
    angles = (indices[:, None] * indices[None, :] % extent) * (2.0 * math.pi / extent)
    norming = 1.0 / math.sqrt(extent)
    return (np.cos(angles) * norming).astype(np.float32), (-np.sin(angles) * norming).astype(np.float32)


def block_table(re, im):
    return jnp.concatenate(
        [jnp.concatenate([re, -im], axis=1), jnp.concatenate([im, re], axis=1)], axis=0
    ).astype(BF)


def make_tables(transfer_phase, extent):
    four_re, four_im = (jnp.asarray(item) for item in fourier(extent))
    cos_phase = jnp.cos(transfer_phase)[:, None]
    sin_phase = jnp.sin(transfer_phase)[:, None]
    mid_re = cos_phase * four_re - sin_phase * four_im
    mid_im = cos_phase * four_im + sin_phase * four_re
    highest = lax.Precision.HIGHEST
    prop_re = jnp.dot(four_re, mid_re, precision=highest) + jnp.dot(four_im, mid_im, precision=highest)
    prop_im = jnp.dot(four_re, mid_im, precision=highest) - jnp.dot(four_im, mid_re, precision=highest)
    return (
        block_table(four_re, four_im),
        block_table(four_re, -four_im),
        block_table(prop_re, prop_im),
        block_table(prop_re.T, -prop_im.T),
    )


def product(left, right):
    return jnp.dot(left, right, preferred_element_type=F32)


def stage_kernel(
    plan, stage, *refs
):
    (first_tile, end_tile, final_tile, halo_start, has_past, is_last, group_tile, group_goes_on) = plan
    refs = list(refs)
    row_ref, col_ref, count_ref = refs[:3]
    del refs[:3]
    four_ref, conj_ref, prop_ref, back_ref = refs[:4]
    del refs[:4]
    probe_ref, intensity_ref, specimen_ref = refs[:3]
    del refs[:3]
    halo_now = refs.pop(0)
    if has_past:
        halo_past, carry_in, probe_in = refs[:3]
        del refs[:4]
    if group_goes_on:
        del refs[:1]
    interior_ref = refs.pop(0)
    overflow_ref = refs.pop(0)
    carry_out = None if is_last else refs.pop(0)
    probe_out = refs.pop(0)
    (slots_ref, ext_ref, acc_ref, measured_ref, round_ref, twice_ref, sum_ref, win_ref, wave0_ref, wave1_ref,
     stack_ref, half_ref, tile_ref, load_sem, slot_sem, store_sem) = refs
    extent = probe_ref.shape[1]
    tiles = end_tile - first_tile
    past_tiles = halo_start - first_tile
    own_count = count_ref[0]
    slot_total = row_ref.shape[0]

    copies = []
    for j in range(tiles):
        lanes = pl.ds((first_tile + j) * LANES, LANES)
        copies.append(pltpu.make_async_copy(
            specimen_ref.at[:, :, :, lanes], ext_ref.at[:, :, j, pl.ds(0, extent), :], load_sem.at[2 * j]))
        if j < past_tiles:
            at = halo_past.shape[3] - (past_tiles - j) * LANES
            source = halo_past.at[:, :, :, pl.ds(at, LANES)]
        else:
            source = halo_now.at[:, :, :, pl.ds((j - past_tiles) * LANES, LANES)]
        copies.append(pltpu.make_async_copy(
            source, ext_ref.at[:, :, j, pl.ds(extent, extent), :], load_sem.at[2 * j + 1]))
    for copy in copies:
        copy.start()
    carried = None
    if has_past:
        carried = pltpu.make_async_copy(carry_in, acc_ref.at[:, :, pl.ds(0, past_tiles), :, :], store_sem.at[0])
        carried.start()

    def gather(k, n):
        last = (col_ref[k] + extent - 1) // LANES
        here = (last >= halo_start) & (last < end_tile) & (k < own_count)

        @pl.when(here)
        def _():
            slots_ref[n] = k

        return n + here.astype(jnp.int32)

    n_slots = lax.fori_loop(0, slot_total, gather, jnp.int32(0))

    def fetch(i):
        return pltpu.make_async_copy(
            intensity_ref.at[slots_ref[i]], measured_ref.at[lax.rem(i, 4)], slot_sem.at[lax.rem(i, 4)])

    def fetch_pair(i):
        for g in range(2):
            @pl.when(i + g < n_slots)
            def _():
                fetch(i + g).start()

    fetch_pair(0)

    for part in range(2):
        for j in range(2):
            block = probe_ref[part, :, j * LANES:(j + 1) * LANES]
            twice_ref[part, j, pl.ds(0, extent), :] = block
            twice_ref[part, j, pl.ds(extent, extent), :] = block
    sum_ref[...] = jnp.zeros_like(sum_ref)
    for j in range(tiles):
        if not (has_past and j < past_tiles):
            acc_ref[:, :, j] = jnp.zeros_like(acc_ref[:, :, j])
    for copy in copies:
        copy.wait()
    if carried is not None:
        carried.wait()

    lane = lax.broadcasted_iota(jnp.int32, (extent, LANES), 1)

    def visit(i, many):
        places = []
        for g in range(many):
            slot = slots_ref[i + g]
            r = row_ref[slot]
            c = col_ref[slot]
            b = c // LANES
            at0 = b - first_tile
            places.append((r, c - b * LANES, (at0, at0 + 1, jnp.minimum(at0 + 2, tiles - 1))))
        every = range(many)

        def row_starts(r):
            return [pl.multiple_of(jnp.where(t + 16 <= r, t + extent, t), 16) for t in range(0, extent, 16)]

        def masks(r, shift):
            mixed = pl.multiple_of(r // 16 * 16, 16)
            low = lax.broadcasted_iota(jnp.int32, (16, LANES), 1) < shift
            own = lax.broadcasted_iota(jnp.int32, (16, LANES), 0) + mixed >= r
            return mixed, low, own

        def take_window(g, s):
            r, shift, ats = places[g]
            at0, at1, at2 = ats
            mixed, low, own = masks(r, shift)
            row_at = row_starts(r)
            for part in range(2):
                for t, at in zip(range(0, extent, 16), row_at):
                    rows = pl.ds(at, 16)
                    win_ref[g, part, s, t:t + 16, 0:LANES] = jnp.where(
                        low, ext_ref[part, s, at2, rows, :], ext_ref[part, s, at0, rows, :])
                    win_ref[g, part, s, t:t + 16, LANES:2 * LANES] = ext_ref[part, s, at1, rows, :]
                rows, rows_under = pl.ds(mixed, 16), pl.ds(pl.multiple_of(mixed + extent, 16), 16)
                picked = [jnp.where(own, ext_ref[part, s, at, rows, :], ext_ref[part, s, at, rows_under, :])
                          for at in ats]
                win_ref[g, part, s, rows, 0:LANES] = jnp.where(low, picked[2], picked[0])
                win_ref[g, part, s, rows, LANES:2 * LANES] = picked[1]

        def take_probe(g):
            r, shift, _ = places[g]
            low = lane < shift
            for part in range(2):
                left = pltpu.roll(twice_ref[part, 0, pl.ds(extent - r, extent), :], shift, 1)
                right = pltpu.roll(twice_ref[part, 1, pl.ds(extent - r, extent), :], shift, 1)
                wave0_ref[g, part, :, 0:LANES] = jnp.where(low, right, left)
                wave0_ref[g, part, :, LANES:2 * LANES] = jnp.where(low, left, right)

        def put(g, re, im):
            lanes = slice(g * extent, (g + 1) * extent)
            stack_ref[0:extent, lanes] = re.astype(BF)
            stack_ref[extent:2 * extent, lanes] = im.astype(BF)

        def leave(wave_ref, s, g):
            spec_re = win_ref[g, 0, s].astype(F32)
            spec_im = win_ref[g, 1, s].astype(F32)
            wave_re, wave_im = wave_ref[g, 0], wave_ref[g, 1]
            put(g, wave_re * spec_re - wave_im * spec_im, wave_re * spec_im + wave_im * spec_re)

        def return_through(wave_ref, s, g, grad_re, grad_im):
            wave_re, wave_im = wave_ref[g, 0], wave_ref[g, 1]
            tile_ref[g, 0, s] = (wave_re * grad_re + wave_im * grad_im).astype(BF)
            tile_ref[g, 1, s] = (wave_re * grad_im - wave_im * grad_re).astype(BF)
            spec_re = win_ref[g, 0, s].astype(F32)
            spec_im = win_ref[g, 1, s].astype(F32)
            return spec_re * grad_re + spec_im * grad_im, spec_re * grad_im - spec_im * grad_re

        def transform(left_ref, right_ref, beside=None):
            wide = product(left_ref[...], stack_ref[:, 0:many * extent])
            for g in every:
                half = wide[:, g * extent:(g + 1) * extent]
                half_ref[g * extent:(g + 1) * extent, 0:extent] = half[:extent].astype(BF)
                half_ref[g * extent:(g + 1) * extent, extent:2 * extent] = half[extent:].astype(BF)
                if beside is not None:
                    beside(g)
            whole = product(half_ref[0:many * extent], right_ref[...])
            return [(whole[g * extent:(g + 1) * extent, :extent], whole[g * extent:(g + 1) * extent, extent:])
                    for g in every]

        def give_probe(g, back):
            r, shift, _ = places[g]
            unroll = lax.rem(LANES - shift, LANES)
            low = lane < LANES - shift
            rows = pl.ds(extent - r, extent)
            for part in range(2):
                left = pltpu.roll(back[part][:, :LANES], unroll, 1)
                right = pltpu.roll(back[part][:, LANES:], unroll, 1)
                sum_ref[part, 0, rows, :] += jnp.where(low, left, right)
                sum_ref[part, 1, rows, :] += jnp.where(low, right, left)

        def give_tile(g, s):
            r, shift, ats = places[g]
            at0, at1, at2 = ats
            mixed, low, own = masks(r, shift)

            def add_rows(part, at, outer, inner):
                rows = pl.ds(at, 16)
                acc_ref[part, s, at0, rows, :] += jnp.where(low, 0.0, outer)
                acc_ref[part, s, at1, rows, :] += inner
                acc_ref[part, s, at2, rows, :] += jnp.where(low, outer, 0.0)

            for part in range(2):
                rows = pl.ds(mixed, 16)
                outer = tile_ref[g, part, s, rows, 0:LANES].astype(F32)
                inner = tile_ref[g, part, s, rows, LANES:2 * LANES].astype(F32)
                add_rows(part, pl.multiple_of(mixed + extent, 16),
                         jnp.where(own, 0.0, outer), jnp.where(own, 0.0, inner))
                tile_ref[g, part, s, rows, 0:LANES] = jnp.where(own, outer, 0.0).astype(BF)
                tile_ref[g, part, s, rows, LANES:2 * LANES] = jnp.where(own, inner, 0.0).astype(BF)
                for t, at in zip(range(0, extent, 16), row_starts(r)):
                    add_rows(part, at, tile_ref[g, part, s, t:t + 16, 0:LANES].astype(F32),
                             tile_ref[g, part, s, t:t + 16, LANES:2 * LANES].astype(F32))

        for g in every:
            take_window(g, 0)
            take_probe(g)
            leave(wave0_ref, 0, g)
        for g, (re, im) in enumerate(transform(prop_ref, back_ref, lambda g: take_window(g, 1))):
            wave1_ref[g, 0] = re
            wave1_ref[g, 1] = im
            leave(wave1_ref, 1, g)
        far = transform(four_ref, conj_ref)
        for g in every:
            fetch(i + g).wait()
        for g, (re, im) in enumerate(far):
            residual = re * re + im * im - measured_ref[lax.rem(i + g, 4)].astype(F32)
            put(g, residual * re, residual * im)
        for g, (re, im) in enumerate(transform(conj_ref, four_ref)):
            put(g, *return_through(wave1_ref, 1, g, re, im))
        grads = transform(back_ref, prop_ref, lambda g: give_tile(g, 1))
        for g, (re, im) in enumerate(grads):
            give_probe(g, return_through(wave0_ref, 0, g, re, im))
        for g in every:
            give_tile(g, 0)

    def visit_pair(p, unused):
        fetch_pair(2 * p + 2)
        visit(2 * p, 2)
        return unused

    lax.fori_loop(0, n_slots // 2, visit_pair, 0)

    @pl.when(lax.rem(n_slots, 2) == 1)
    def _():
        visit(n_slots - 1, 1)

    copies = []
    done_tiles = final_tile - first_tile
    for j in range(done_tiles):
        lanes = pl.ds((first_tile + j) * LANES, LANES)
        copies.append(pltpu.make_async_copy(
            acc_ref.at[:, :, j, pl.ds(0, extent), :], interior_ref.at[:, :, :, lanes], load_sem.at[2 * j]))
        copies[-1].start()
        round_ref[:, :, j] = acc_ref[:, :, j, extent:2 * extent, :].astype(BF)
        copies.append(pltpu.make_async_copy(
            round_ref.at[:, :, j], overflow_ref.at[:, :, :, pl.ds((first_tile - group_tile + j) * LANES, LANES)],
            load_sem.at[2 * j + 1]))
        copies[-1].start()
    if carry_out is not None:
        copies.append(pltpu.make_async_copy(
            acc_ref.at[:, :, pl.ds(done_tiles, tiles - done_tiles), :, :], carry_out, store_sem.at[0]))
        copies[-1].start()
    for part in range(2):
        for j in range(2):
            term = sum_ref[part, j, 0:extent, :] + sum_ref[part, j, extent:2 * extent, :]
            if has_past:
                term = term + probe_in[part, :, j * LANES:(j + 1) * LANES]
            probe_out[part, :, j * LANES:(j + 1) * LANES] = term
    for copy in copies:
        copy.wait()


def run_stage(stage, ends, group, meta, tables, probe_field, intensity, specimen, halos, past):
    slices, block_rows, columns = specimen.shape[1:]
    extent = probe_field.shape[1]
    is_last = stage == len(ends) - 1
    has_past = stage > 0
    halo_start = ends[stage - 1] if has_past else 0
    first_tile = max(halo_start - 2, 0) if has_past else 0
    end_tile = ends[stage]
    final_tile = end_tile if is_last else end_tile - 2
    tiles = end_tile - first_tile
    group_tile, group_end, overflow = group
    group_goes_on = overflow is not None
    plan = (first_tile, end_tile, final_tile, halo_start, has_past, is_last, group_tile, group_goes_on)
    smem = pl.BlockSpec(memory_space=pltpu.SMEM)
    vmem = pl.BlockSpec(memory_space=pltpu.VMEM)
    hbm = pl.BlockSpec(memory_space=pltpu.HBM)
    free = pl.BlockSpec(memory_space=pl.ANY)
    args = [*meta, *tables, probe_field, intensity, specimen, halos[stage]]
    in_specs = [smem] * 3 + [vmem] * 4 + [vmem, hbm, hbm, free]
    aliases = {}
    if has_past:
        interior, carry, probe_sum = past
        args += [halos[stage - 1], carry, probe_sum, interior]
        in_specs += [free, hbm, vmem, hbm]
        aliases = {len(args) - 1: 0}
    if group_goes_on:
        args += [overflow]
        in_specs += [hbm]
        aliases[len(args) - 1] = 1
    outs = [
        jax.ShapeDtypeStruct((2, slices, block_rows, columns), F32),
        jax.ShapeDtypeStruct((2, slices, extent, (group_end - group_tile) * LANES), BF),
    ]
    out_specs = [hbm, hbm]
    if not is_last:
        outs.append(jax.ShapeDtypeStruct((2, slices, end_tile - final_tile, 2 * extent, LANES), F32))
        out_specs.append(hbm)
    outs.append(jax.ShapeDtypeStruct((2, extent, extent), F32))
    out_specs.append(vmem)
    pairs = (2, slices)
    scratch = [
        pltpu.SMEM((meta[0].shape[0],), jnp.int32),
        pltpu.VMEM((*pairs, tiles, 2 * extent, LANES), BF),
        pltpu.VMEM((*pairs, tiles, 2 * extent, LANES), F32),
        pltpu.VMEM((4, extent, extent), BF),
        pltpu.VMEM((*pairs, max(final_tile - first_tile, 1), extent, LANES), BF),
        pltpu.VMEM((2, 2, 2 * extent, LANES), F32),
        pltpu.VMEM((2, 2, 2 * extent, LANES), F32),
        pltpu.VMEM((2, *pairs, extent, extent), BF),
        pltpu.VMEM((2, 2, extent, extent), F32),
        pltpu.VMEM((2, 2, extent, extent), F32),
        pltpu.VMEM((2 * extent, 2 * extent), BF),
        pltpu.VMEM((2 * extent, 2 * extent), BF),
        pltpu.VMEM((2, *pairs, extent, extent), BF),
        pltpu.SemaphoreType.DMA((2 * tiles,)),
        pltpu.SemaphoreType.DMA((4,)),
        pltpu.SemaphoreType.DMA((1,)),
    ]
    results = list(pl.pallas_call(
        functools.partial(stage_kernel, plan, stage),
        out_shape=outs,
        in_specs=in_specs,
        out_specs=out_specs,
        scratch_shapes=scratch,
        input_output_aliases=aliases,
        compiler_params=pltpu.CompilerParams(vmem_limit_bytes=50 * 1024 * 1024),
        cost_estimate=pl.CostEstimate(flops=3 * 10**9, bytes_accessed=8 * 10**6, transcendentals=0),
        name=f"stage{stage}",
    )(*args))
    interior = results.pop(0)
    overflow = results.pop(0)
    carry = None if is_last else results.pop(0)
    return (interior, carry, results.pop(0)), (group_tile, group_end, overflow)


def add_kernel(first_tile, tiles, held_ref, came_ref, out_ref, held, came, in_sem, out_sem):
    def copies(j):
        lanes = pl.ds((first_tile + j) * LANES, LANES)
        return (
            pltpu.make_async_copy(held_ref.at[:, :, :, lanes], held.at[j], in_sem.at[2 * j]),
            pltpu.make_async_copy(came_ref.at[:, :, :, pl.ds(j * LANES, LANES)], came.at[j], in_sem.at[2 * j + 1]),
            pltpu.make_async_copy(held.at[j], out_ref.at[:, :, :, lanes], out_sem.at[j]),
        )

    for j in range(tiles):
        for copy in copies(j)[:2]:
            copy.start()
    for j in range(tiles):
        for copy in copies(j)[:2]:
            copy.wait()
        held[j] = held[j] + came[j].astype(F32)
        copies(j)[2].start()
    for j in range(tiles):
        copies(j)[2].wait()


def add_chunk(interior, came, first_tile):
    _, slices, rows, _ = interior.shape
    tiles = came.shape[3] // LANES
    hbm = pl.BlockSpec(memory_space=pltpu.HBM)
    block = (tiles, 2, slices, rows, LANES)
    return pl.pallas_call(
        functools.partial(add_kernel, first_tile, tiles),
        out_shape=jax.ShapeDtypeStruct(interior.shape, interior.dtype),
        in_specs=[hbm, pl.BlockSpec(memory_space=pl.ANY)],
        out_specs=hbm,
        scratch_shapes=[
            pltpu.VMEM(block, F32),
            pltpu.VMEM(block, BF),
            pltpu.SemaphoreType.DMA((2 * tiles,)),
            pltpu.SemaphoreType.DMA((tiles,)),
        ],
        input_output_aliases={0: 0},
        compiler_params=pltpu.CompilerParams(vmem_limit_bytes=50 * 1024 * 1024),
        name=f"add{first_tile}",
    )(interior, came)


def exchanged(value, axis, step):
    return lax.ppermute(value, axis, [(k, k ^ step) for k in range(lax.axis_size(axis))])


def sum_over(value, axis, meanwhile):
    count = lax.axis_size(axis)
    steps = [1 << k for k in range(1, count.bit_length() - 1)]
    odd = lax.rem(lax.axis_index(axis), 2) == 1
    kept, given = jnp.where(odd, value[1], value[0]), jnp.where(odd, value[0], value[1])
    kept = kept.astype(BF).astype(F32) + exchanged(given.astype(BF), axis, 1).astype(F32)
    for n in range(1, len(steps), 2):
        mine = kept.astype(BF)
        kept = mine.astype(F32) + exchanged(mine, axis, steps[n]).astype(F32)
        if n + 1 < len(steps):
            far, across = (exchanged(mine, axis, step) for step in (steps[n + 1], steps[n] ^ steps[n + 1]))
            kept = kept + (far.astype(F32) + across.astype(F32))
    kept = meanwhile(kept)
    for step in steps[:1]:
        mine = kept.astype(BF)
        kept = mine.astype(F32) + exchanged(mine, axis, step).astype(F32)
    other = exchanged(kept, axis, 1)
    return jnp.stack([jnp.where(odd, other, kept), jnp.where(odd, kept, other)])


def body(ends, sends, specimen, probe_field, transfer_phase, intensity, row_offset, col_offset, counts):
    extent = probe_field.shape[1]
    tables = make_tables(transfer_phase, extent)
    halos, source, start = [], specimen, 0
    for k, end in enumerate(ends):
        piece = source[:, :, :, start * LANES:end * LANES]
        halos.append(passed_along(piece, "row", -1))
        start = end
    meta = (row_offset, col_offset, counts)
    past, sent, at = None, [], 0
    for stage in range(len(ends)):
        if stage == 0 or stage - 1 in sends:
            last = min(send for send in sends if send >= stage)
            until = ends[last] if last == len(ends) - 1 else ends[last] - 2
            group = (at, until, None)
        past, group = run_stage(
            stage, ends, group, meta, tables, probe_field, intensity, specimen, halos, past)
        if stage in sends:
            if stage + 1 < len(ends):
                ready, halos[stage + 1] = lax.optimization_barrier((group[2], halos[stage + 1]))
                group = (*group[:2], ready)
            sent.append((group[2], group[0]))
            at = group[1]
    interior, _, probe_sum = past
    came = [(passed_along(chunk, "row", 1), first) for chunk, first in sent]
    held = []

    def meanwhile(kept):
        kept, first = lax.optimization_barrier((kept, add_chunk(interior, *came[0])))
        held.append(first)
        return kept

    probe_total = sum_over(probe_sum, "row", meanwhile)
    interior = add_chunk(held[0], *came[1])
    return interior, probe_total


def solution(mesh):
    return jax.shard_map(
        functools.partial(body, (5, 11, 16), (1, 2)),
        mesh=mesh,
        in_specs=(
            P("group", None, "row", None),
            P("group", None, None),
            P(),
            P(("group", "row"), None, None),
            P(("group", "row")),
            P(("group", "row")),
            P(("group", "row")),
        ),
        out_specs=(P("group", None, "row", None), P("group", None, None)),
        check_vma=False,
    )
```

```python
import functools
import math

import jax
import jax.numpy as jnp
import numpy as np
from jax import lax
from jax.experimental import pallas as pl
from jax.experimental.pallas import tpu as pltpu
from jax.sharding import PartitionSpec as P

LANES = 128
BF = jnp.bfloat16
F32 = jnp.float32


def passed_along(value, axis, steps):
    count = lax.axis_size(axis)
    first, last = (max(0, -steps), min(count, count - steps))
    return lax.ppermute(value, axis, [(source, source + steps) for source in range(first, last)])


def fourier(extent):
    indices = np.arange(extent, dtype=np.int64)
    angles = (indices[:, None] * indices[None, :] % extent) * (2.0 * math.pi / extent)
    norming = 1.0 / math.sqrt(extent)
    return (np.cos(angles) * norming).astype(np.float32), (-np.sin(angles) * norming).astype(np.float32)


def block_table(re, im):
    return jnp.concatenate(
        [jnp.concatenate([re, -im], axis=1), jnp.concatenate([im, re], axis=1)], axis=0
    ).astype(BF)


def make_tables(transfer_phase, extent):
    four_re, four_im = (jnp.asarray(item) for item in fourier(extent))
    cos_phase = jnp.cos(transfer_phase)[:, None]
    sin_phase = jnp.sin(transfer_phase)[:, None]
    mid_re = cos_phase * four_re - sin_phase * four_im
    mid_im = cos_phase * four_im + sin_phase * four_re
    highest = lax.Precision.HIGHEST
    prop_re = jnp.dot(four_re, mid_re, precision=highest) + jnp.dot(four_im, mid_im, precision=highest)
    prop_im = jnp.dot(four_re, mid_im, precision=highest) - jnp.dot(four_im, mid_re, precision=highest)
    return (
        block_table(four_re, four_im),
        block_table(four_re, -four_im),
        block_table(prop_re, prop_im),
        block_table(prop_re.T, -prop_im.T),
    )


def product(left, right):
    return jnp.dot(left, right, preferred_element_type=F32)


def stage_kernel(
    plan, stage, *refs
):
    (first_tile, end_tile, final_tile, halo_start, has_past, is_last, group_tile, group_goes_on) = plan
    refs = list(refs)
    row_ref, col_ref, count_ref = refs[:3]
    del refs[:3]
    four_ref, conj_ref, prop_ref, back_ref = refs[:4]
    del refs[:4]
    probe_ref, intensity_ref, specimen_ref = refs[:3]
    del refs[:3]
    halo_now = refs.pop(0)
    if has_past:
        halo_past, carry_in, probe_in = refs[:3]
        del refs[:4]
    if group_goes_on:
        del refs[:1]
    interior_ref = refs.pop(0)
    overflow_ref = refs.pop(0)
    carry_out = None if is_last else refs.pop(0)
    probe_out = refs.pop(0)
    (slots_ref, ext_ref, acc_ref, measured_ref, round_ref, twice_ref, sum_ref, win_ref, wave0_ref, wave1_ref,
     stack_ref, half_ref, tile_ref, load_sem, slot_sem, store_sem) = refs
    extent = probe_ref.shape[1]
    tiles = end_tile - first_tile
    past_tiles = halo_start - first_tile
    own_count = count_ref[0]
    slot_total = row_ref.shape[0]

    copies = []
    for j in range(tiles):
        lanes = pl.ds((first_tile + j) * LANES, LANES)
        copies.append(pltpu.make_async_copy(
            specimen_ref.at[:, :, :, lanes], ext_ref.at[:, :, j, pl.ds(0, extent), :], load_sem.at[2 * j]))
        if j < past_tiles:
            at = halo_past.shape[3] - (past_tiles - j) * LANES
            source = halo_past.at[:, :, :, pl.ds(at, LANES)]
        else:
            source = halo_now.at[:, :, :, pl.ds((j - past_tiles) * LANES, LANES)]
        copies.append(pltpu.make_async_copy(
            source, ext_ref.at[:, :, j, pl.ds(extent, extent), :], load_sem.at[2 * j + 1]))
    for copy in copies:
        copy.start()
    carried = None
    if has_past:
        carried = pltpu.make_async_copy(carry_in, acc_ref.at[:, :, pl.ds(0, past_tiles), :, :], store_sem.at[0])
        carried.start()

    def gather(k, n):
        last = (col_ref[k] + extent - 1) // LANES
        here = (last >= halo_start) & (last < end_tile) & (k < own_count)

        @pl.when(here)
        def _():
            slots_ref[n] = k

        return n + here.astype(jnp.int32)

    n_slots = lax.fori_loop(0, slot_total, gather, jnp.int32(0))

    def fetch(i):
        return pltpu.make_async_copy(
            intensity_ref.at[slots_ref[i]], measured_ref.at[lax.rem(i, 4)], slot_sem.at[lax.rem(i, 4)])

    def fetch_pair(i):
        for g in range(2):
            @pl.when(i + g < n_slots)
            def _():
                fetch(i + g).start()

    fetch_pair(0)

    for part in range(2):
        for j in range(2):
            block = probe_ref[part, :, j * LANES:(j + 1) * LANES]
            twice_ref[part, j, pl.ds(0, extent), :] = block
            twice_ref[part, j, pl.ds(extent, extent), :] = block
    sum_ref[...] = jnp.zeros_like(sum_ref)
    for j in range(tiles):
        if not (has_past and j < past_tiles):
            acc_ref[:, :, j] = jnp.zeros_like(acc_ref[:, :, j])
    for copy in copies:
        copy.wait()
    if carried is not None:
        carried.wait()

    lane = lax.broadcasted_iota(jnp.int32, (extent, LANES), 1)

    def visit(i, many):
        places = []
        for g in range(many):
            slot = slots_ref[i + g]
            r = row_ref[slot]
            c = col_ref[slot]
            b = c // LANES
            at0 = b - first_tile
            places.append((r, c - b * LANES, (at0, at0 + 1, jnp.minimum(at0 + 2, tiles - 1))))
        every = range(many)

        def row_starts(r):
            return [pl.multiple_of(jnp.where(t + 16 <= r, t + extent, t), 16) for t in range(0, extent, 16)]

        def masks(r, shift):
            mixed = pl.multiple_of(r // 16 * 16, 16)
            low = lax.broadcasted_iota(jnp.int32, (16, LANES), 1) < shift
            own = lax.broadcasted_iota(jnp.int32, (16, LANES), 0) + mixed >= r
            return mixed, low, own

        def take_window(g, s):
            r, shift, ats = places[g]
            at0, at1, at2 = ats
            mixed, low, own = masks(r, shift)
            row_at = row_starts(r)
            for part in range(2):
                for t, at in zip(range(0, extent, 16), row_at):
                    rows = pl.ds(at, 16)
                    win_ref[g, part, s, t:t + 16, 0:LANES] = jnp.where(
                        low, ext_ref[part, s, at2, rows, :], ext_ref[part, s, at0, rows, :])
                    win_ref[g, part, s, t:t + 16, LANES:2 * LANES] = ext_ref[part, s, at1, rows, :]
                rows, rows_under = pl.ds(mixed, 16), pl.ds(pl.multiple_of(mixed + extent, 16), 16)
                picked = [jnp.where(own, ext_ref[part, s, at, rows, :], ext_ref[part, s, at, rows_under, :])
                          for at in ats]
                win_ref[g, part, s, rows, 0:LANES] = jnp.where(low, picked[2], picked[0])
                win_ref[g, part, s, rows, LANES:2 * LANES] = picked[1]

        def take_probe(g):
            r, shift, _ = places[g]
            low = lane < shift
            for part in range(2):
                left = pltpu.roll(twice_ref[part, 0, pl.ds(extent - r, extent), :], shift, 1)
                right = pltpu.roll(twice_ref[part, 1, pl.ds(extent - r, extent), :], shift, 1)
                wave0_ref[g, part, :, 0:LANES] = jnp.where(low, right, left)
                wave0_ref[g, part, :, LANES:2 * LANES] = jnp.where(low, left, right)

        def put(g, re, im):
            lanes = slice(g * extent, (g + 1) * extent)
            stack_ref[0:extent, lanes] = re.astype(BF)
            stack_ref[extent:2 * extent, lanes] = im.astype(BF)

        def leave(wave_ref, s, g):
            spec_re = win_ref[g, 0, s].astype(F32)
            spec_im = win_ref[g, 1, s].astype(F32)
            wave_re, wave_im = wave_ref[g, 0], wave_ref[g, 1]
            put(g, wave_re * spec_re - wave_im * spec_im, wave_re * spec_im + wave_im * spec_re)

        def return_through(wave_ref, s, g, grad_re, grad_im):
            wave_re, wave_im = wave_ref[g, 0], wave_ref[g, 1]
            tile_ref[g, 0, s] = (wave_re * grad_re + wave_im * grad_im).astype(BF)
            tile_ref[g, 1, s] = (wave_re * grad_im - wave_im * grad_re).astype(BF)
            spec_re = win_ref[g, 0, s].astype(F32)
            spec_im = win_ref[g, 1, s].astype(F32)
            return spec_re * grad_re + spec_im * grad_im, spec_re * grad_im - spec_im * grad_re

        def transform(left_ref, right_ref, beside=None):
            wide = product(left_ref[...], stack_ref[:, 0:many * extent])
            for g in every:
                half = wide[:, g * extent:(g + 1) * extent]
                half_ref[g * extent:(g + 1) * extent, 0:extent] = half[:extent].astype(BF)
                half_ref[g * extent:(g + 1) * extent, extent:2 * extent] = half[extent:].astype(BF)
                if beside is not None:
                    beside(g)
            whole = product(half_ref[0:many * extent], right_ref[...])
            return [(whole[g * extent:(g + 1) * extent, :extent], whole[g * extent:(g + 1) * extent, extent:])
                    for g in every]

        def give_probe(g, back):
            r, shift, _ = places[g]
            unroll = lax.rem(LANES - shift, LANES)
            low = lane < LANES - shift
            rows = pl.ds(extent - r, extent)
            for part in range(2):
                left = pltpu.roll(back[part][:, :LANES], unroll, 1)
                right = pltpu.roll(back[part][:, LANES:], unroll, 1)
                sum_ref[part, 0, rows, :] += jnp.where(low, left, right)
                sum_ref[part, 1, rows, :] += jnp.where(low, right, left)

        def give_tile(g, s):
            r, shift, ats = places[g]
            at0, at1, at2 = ats
            mixed, low, own = masks(r, shift)

            def add_rows(part, at, outer, inner):
                rows = pl.ds(at, 16)
                acc_ref[part, s, at0, rows, :] += jnp.where(low, 0.0, outer)
                acc_ref[part, s, at1, rows, :] += inner
                acc_ref[part, s, at2, rows, :] += jnp.where(low, outer, 0.0)

            for part in range(2):
                rows = pl.ds(mixed, 16)
                outer = tile_ref[g, part, s, rows, 0:LANES].astype(F32)
                inner = tile_ref[g, part, s, rows, LANES:2 * LANES].astype(F32)
                add_rows(part, pl.multiple_of(mixed + extent, 16),
                         jnp.where(own, 0.0, outer), jnp.where(own, 0.0, inner))
                tile_ref[g, part, s, rows, 0:LANES] = jnp.where(own, outer, 0.0).astype(BF)
                tile_ref[g, part, s, rows, LANES:2 * LANES] = jnp.where(own, inner, 0.0).astype(BF)
                for t, at in zip(range(0, extent, 16), row_starts(r)):
                    add_rows(part, at, tile_ref[g, part, s, t:t + 16, 0:LANES].astype(F32),
                             tile_ref[g, part, s, t:t + 16, LANES:2 * LANES].astype(F32))

        for g in every:
            take_window(g, 0)
            take_probe(g)
            leave(wave0_ref, 0, g)
        for g, (re, im) in enumerate(transform(prop_ref, back_ref, lambda g: take_window(g, 1))):
            wave1_ref[g, 0] = re
            wave1_ref[g, 1] = im
            leave(wave1_ref, 1, g)
        far = transform(four_ref, conj_ref)
        for g in every:
            fetch(i + g).wait()
        for g, (re, im) in enumerate(far):
            residual = re * re + im * im - measured_ref[lax.rem(i + g, 4)].astype(F32)
            put(g, residual * re, residual * im)
        for g, (re, im) in enumerate(transform(conj_ref, four_ref)):
            put(g, *return_through(wave1_ref, 1, g, re, im))
        grads = transform(back_ref, prop_ref, lambda g: give_tile(g, 1))
        for g, (re, im) in enumerate(grads):
            give_probe(g, return_through(wave0_ref, 0, g, re, im))
        for g in every:
            give_tile(g, 0)

    def visit_pair(p, unused):
        fetch_pair(2 * p + 2)
        visit(2 * p, 2)
        return unused

    lax.fori_loop(0, n_slots // 2, visit_pair, 0)

    @pl.when(lax.rem(n_slots, 2) == 1)
    def _():
        visit(n_slots - 1, 1)

    copies = []
    done_tiles = final_tile - first_tile
    for j in range(done_tiles):
        lanes = pl.ds((first_tile + j) * LANES, LANES)
        copies.append(pltpu.make_async_copy(
            acc_ref.at[:, :, j, pl.ds(0, extent), :], interior_ref.at[:, :, :, lanes], load_sem.at[2 * j]))
        copies[-1].start()
        round_ref[:, :, j] = acc_ref[:, :, j, extent:2 * extent, :].astype(BF)
        copies.append(pltpu.make_async_copy(
            round_ref.at[:, :, j], overflow_ref.at[:, :, :, pl.ds((first_tile - group_tile + j) * LANES, LANES)],
            load_sem.at[2 * j + 1]))
        copies[-1].start()
    if carry_out is not None:
        copies.append(pltpu.make_async_copy(
            acc_ref.at[:, :, pl.ds(done_tiles, tiles - done_tiles), :, :], carry_out, store_sem.at[0]))
        copies[-1].start()
    for part in range(2):
        for j in range(2):
            term = sum_ref[part, j, 0:extent, :] + sum_ref[part, j, extent:2 * extent, :]
            if has_past:
                term = term + probe_in[part, :, j * LANES:(j + 1) * LANES]
            probe_out[part, :, j * LANES:(j + 1) * LANES] = term
    for copy in copies:
        copy.wait()


def run_stage(stage, ends, group, meta, tables, probe_field, intensity, specimen, halos, past):
    slices, block_rows, columns = specimen.shape[1:]
    extent = probe_field.shape[1]
    is_last = stage == len(ends) - 1
    has_past = stage > 0
    halo_start = ends[stage - 1] if has_past else 0
    first_tile = max(halo_start - 2, 0) if has_past else 0
    end_tile = ends[stage]
    final_tile = end_tile if is_last else end_tile - 2
    tiles = end_tile - first_tile
    group_tile, group_end, overflow = group
    group_goes_on = overflow is not None
    plan = (first_tile, end_tile, final_tile, halo_start, has_past, is_last, group_tile, group_goes_on)
    smem = pl.BlockSpec(memory_space=pltpu.SMEM)
    vmem = pl.BlockSpec(memory_space=pltpu.VMEM)
    hbm = pl.BlockSpec(memory_space=pltpu.HBM)
    free = pl.BlockSpec(memory_space=pl.ANY)
    args = [*meta, *tables, probe_field, intensity, specimen, halos[stage]]
    in_specs = [smem] * 3 + [vmem] * 4 + [vmem, hbm, hbm, free]
    aliases = {}
    if has_past:
        interior, carry, probe_sum = past
        args += [halos[stage - 1], carry, probe_sum, interior]
        in_specs += [free, hbm, vmem, hbm]
        aliases = {len(args) - 1: 0}
    if group_goes_on:
        args += [overflow]
        in_specs += [hbm]
        aliases[len(args) - 1] = 1
    outs = [
        jax.ShapeDtypeStruct((2, slices, block_rows, columns), F32),
        jax.ShapeDtypeStruct((2, slices, extent, (group_end - group_tile) * LANES), BF),
    ]
    out_specs = [hbm, hbm]
    if not is_last:
        outs.append(jax.ShapeDtypeStruct((2, slices, end_tile - final_tile, 2 * extent, LANES), F32))
        out_specs.append(hbm)
    outs.append(jax.ShapeDtypeStruct((2, extent, extent), F32))
    out_specs.append(vmem)
    pairs = (2, slices)
    scratch = [
        pltpu.SMEM((meta[0].shape[0],), jnp.int32),
        pltpu.VMEM((*pairs, tiles, 2 * extent, LANES), BF),
        pltpu.VMEM((*pairs, tiles, 2 * extent, LANES), F32),
        pltpu.VMEM((4, extent, extent), BF),
        pltpu.VMEM((*pairs, max(final_tile - first_tile, 1), extent, LANES), BF),
        pltpu.VMEM((2, 2, 2 * extent, LANES), F32),
        pltpu.VMEM((2, 2, 2 * extent, LANES), F32),
        pltpu.VMEM((2, *pairs, extent, extent), BF),
        pltpu.VMEM((2, 2, extent, extent), F32),
        pltpu.VMEM((2, 2, extent, extent), F32),
        pltpu.VMEM((2 * extent, 2 * extent), BF),
        pltpu.VMEM((2 * extent, 2 * extent), BF),
        pltpu.VMEM((2, *pairs, extent, extent), BF),
        pltpu.SemaphoreType.DMA((2 * tiles,)),
        pltpu.SemaphoreType.DMA((4,)),
        pltpu.SemaphoreType.DMA((1,)),
    ]
    results = list(pl.pallas_call(
        functools.partial(stage_kernel, plan, stage),
        out_shape=outs,
        in_specs=in_specs,
        out_specs=out_specs,
        scratch_shapes=scratch,
        input_output_aliases=aliases,
        compiler_params=pltpu.CompilerParams(vmem_limit_bytes=50 * 1024 * 1024),
        cost_estimate=pl.CostEstimate(flops=3 * 10**9, bytes_accessed=8 * 10**6, transcendentals=0),
        name=f"stage{stage}",
    )(*args))
    interior = results.pop(0)
    overflow = results.pop(0)
    carry = None if is_last else results.pop(0)
    return (interior, carry, results.pop(0)), (group_tile, group_end, overflow)


def add_kernel(first_tile, tiles, held_ref, came_ref, out_ref, held, came, in_sem, out_sem):
    def copies(j):
        lanes = pl.ds((first_tile + j) * LANES, LANES)
        return (
            pltpu.make_async_copy(held_ref.at[:, :, :, lanes], held.at[j], in_sem.at[2 * j]),
            pltpu.make_async_copy(came_ref.at[:, :, :, pl.ds(j * LANES, LANES)], came.at[j], in_sem.at[2 * j + 1]),
            pltpu.make_async_copy(held.at[j], out_ref.at[:, :, :, lanes], out_sem.at[j]),
        )

    for j in range(tiles):
        for copy in copies(j)[:2]:
            copy.start()
    for j in range(tiles):
        for copy in copies(j)[:2]:
            copy.wait()
        held[j] = held[j] + came[j].astype(F32)
        copies(j)[2].start()
    for j in range(tiles):
        copies(j)[2].wait()


def add_chunk(interior, came, first_tile):
    _, slices, rows, _ = interior.shape
    tiles = came.shape[3] // LANES
    hbm = pl.BlockSpec(memory_space=pltpu.HBM)
    block = (tiles, 2, slices, rows, LANES)
    return pl.pallas_call(
        functools.partial(add_kernel, first_tile, tiles),
        out_shape=jax.ShapeDtypeStruct(interior.shape, interior.dtype),
        in_specs=[hbm, pl.BlockSpec(memory_space=pl.ANY)],
        out_specs=hbm,
        scratch_shapes=[
            pltpu.VMEM(block, F32),
            pltpu.VMEM(block, BF),
            pltpu.SemaphoreType.DMA((2 * tiles,)),
            pltpu.SemaphoreType.DMA((tiles,)),
        ],
        input_output_aliases={0: 0},
        compiler_params=pltpu.CompilerParams(vmem_limit_bytes=50 * 1024 * 1024),
        name=f"add{first_tile}",
    )(interior, came)


def exchanged(value, axis, step):
    return lax.ppermute(value, axis, [(k, k ^ step) for k in range(lax.axis_size(axis))])


def sum_over(value, axis):
    count = lax.axis_size(axis)
    steps = [1 << k for k in range(1, count.bit_length() - 1)]
    odd = lax.rem(lax.axis_index(axis), 2) == 1
    kept, given = jnp.where(odd, value[1], value[0]), jnp.where(odd, value[0], value[1])
    kept = kept.astype(BF).astype(F32) + exchanged(given.astype(BF), axis, 1).astype(F32)
    for n in range(1, len(steps), 2):
        mine = kept.astype(BF)
        kept = mine.astype(F32) + exchanged(mine, axis, steps[n]).astype(F32)
        if n + 1 < len(steps):
            far, across = (exchanged(mine, axis, step) for step in (steps[n + 1], steps[n] ^ steps[n + 1]))
            kept = kept + (far.astype(F32) + across.astype(F32))
    for step in steps[:1]:
        mine = kept.astype(BF)
        kept = mine.astype(F32) + exchanged(mine, axis, step).astype(F32)
    other = exchanged(kept, axis, 1)
    return jnp.stack([jnp.where(odd, other, kept), jnp.where(odd, kept, other)])


def body(ends, sends, specimen, probe_field, transfer_phase, intensity, row_offset, col_offset, counts):
    extent = probe_field.shape[1]
    tables = make_tables(transfer_phase, extent)
    halos, source, start = [], specimen, 0
    for k, end in enumerate(ends):
        piece = source[:, :, :, start * LANES:end * LANES]
        halos.append(passed_along(piece, "row", -1))
        start = end
    meta = (row_offset, col_offset, counts)
    past, sent, at = None, [], 0
    for stage in range(len(ends)):
        if stage == 0 or stage - 1 in sends:
            last = min(send for send in sends if send >= stage)
            until = ends[last] if last == len(ends) - 1 else ends[last] - 2
            group = (at, until, None)
        past, group = run_stage(
            stage, ends, group, meta, tables, probe_field, intensity, specimen, halos, past)
        if stage in sends:
            if stage + 1 < len(ends):
                ready, halos[stage + 1] = lax.optimization_barrier((group[2], halos[stage + 1]))
                group = (*group[:2], ready)
            sent.append((group[2], group[0]))
            at = group[1]
    interior, _, probe_sum = past
    came = [(passed_along(chunk, "row", 1), first) for chunk, first in sent]
    interior = add_chunk(interior, *came[0])
    interior, probe_sum = lax.optimization_barrier((interior, probe_sum))
    probe_total = sum_over(probe_sum, "row")
    interior = add_chunk(interior, *came[1])
    return interior, probe_total


def solution(mesh):
    return jax.shard_map(
        functools.partial(body, (5, 10, 16), (1, 2)),
        mesh=mesh,
        in_specs=(
            P("group", None, "row", None),
            P("group", None, None),
            P(),
            P(("group", "row"), None, None),
            P(("group", "row")),
            P(("group", "row")),
            P(("group", "row")),
        ),
        out_specs=(P("group", None, "row", None), P("group", None, None)),
        check_vma=False,
    )
```
